32 devices in a mesh: groups: 2 (over x), exp: 16 (over z, y, core).
Axes of the slice: x: 2, y: 2, z: 4, core: 2. Of those that a mesh axis runs over, the one named last changes fastest.
Arguments:
- estimate: float32 [512, 4, 512], P('exp', 'groups'), parts along dimension 1, may hold values from -6 to 6
- observed: bfloat16 [32, 512, 512], P(('groups', 'exp')), parts along dimension 0, may hold values from -12 to 12
- pixel_mask: int32 [32, 512, 512], P(('groups', 'exp')), parts along dimension 0, may hold values 0 or 1
- blur_mix: float32 [32, 6, 8, 8], P(('groups', 'exp')), parts along dimension 0, may hold values from 0.2 to 1
- dithers: int32 [32, 2], P(('groups', 'exp')), parts along dimension 0, may hold values from -8 to 8, as said below
- patch_of: int32 [32], P(('groups', 'exp')), parts along dimension 0, may hold values from 0 to 1
- column_taps: bfloat16 [6, 15], replicated, may hold values from 0 to 0.119628906
- row_taps: bfloat16 [6, 15], replicated, may hold values from 0 to 0.119628906
Outputs:
- gradient: float32 [512, 4, 512], P('exp', 'groups'), parts along dimension 1
The draws below stay inside these ranges and needn't reach their ends.
There are 2 independent parts, one for each index of `groups`. The reference program is written for one: setup_inputs(seed, part) draws one part's arguments, and reference() takes and returns one part's arrays. A program takes and returns all parts, laid end to end along the dimension named above; an argument that names none is the same for every part. Nothing has to cross between parts.
Inputs may be any that keep to these rules, and one draw needn't show every extreme that they name: `dithers`: each exposure's two offsets; the value 8 occurs among the row offsets and -8 among the column offsets.
All inputs are finite; a program needn't handle non-finite values. No bound on the sum of `pixel_mask` on one device may be relied on, other than what follows from the above.
Results may differ from the reference program's by a relative error of at most 0.004.
Values may be sent and summed in bfloat16 or wider, within the bound.
A program may use at most 128 MiB of HBM per device.

```python
import jax
import jax.numpy as jnp
from jax import lax

PATCH = 512
PATCHES = 2
BASES = 6
TAPS = 15
DMAX = 8
TILES = 8
EXPOSURES = 16


def draw_dithers(key, part):
    base_value = jax.random.randint(jax.random.fold_in(key, 11), (EXPOSURES, 2), -DMAX, DMAX + 1)
    chosen = jax.random.randint(jax.random.fold_in(key, 12), (2,), 0, EXPOSURES)
    row_ids = lax.broadcasted_iota(jnp.int32, (EXPOSURES, 2), 0)
    col_ids = lax.broadcasted_iota(jnp.int32, (EXPOSURES, 2), 1)
    base_value = jnp.where((row_ids == chosen[0]) & (col_ids == 0), DMAX, base_value)
    base_value = jnp.where((row_ids == chosen[1]) & (col_ids == 1), -DMAX, base_value)
    return base_value.astype(jnp.int32)


def set_ends(values, key, smallest, high):
    longest = values.shape.index(max(values.shape))
    spots = []
    for shift in (0, 1):
        where = [jax.random.randint(jax.random.fold_in(key, axis), (), 0, length) for axis, length in enumerate(values.shape)]
        where[longest] = (where[longest] + shift) % values.shape[longest]
        spots.append(tuple(where))
    return values.at[spots[0]].set(smallest).at[spots[1]].set(high)


def shard_levels(stream_key, shape, split, low, top_value):
    factor_of = 1.0
    for axis_at, parts in split:
        steps = jax.random.uniform(jax.random.fold_in(jax.random.fold_in(stream_key, 6), axis_at), (parts,), jnp.float32, low / len(split), top_value / len(split))
        factor_of = factor_of * jnp.repeat(jnp.exp(steps), shape[axis_at] // parts).reshape((-1,) + (1,) * (len(shape) - 1 - axis_at))
    return factor_of


def noise(rng, shape, spread, most, split=(), dtype=jnp.bfloat16):
    values = jax.random.normal(rng, shape, jnp.float32) * spread
    if len(split) > 0:
        values = shard_levels(rng, shape, split, -0.22, 0.18) * values
    return jnp.clip(values, min=-most, max=most).astype(dtype)


def setup_inputs(seed: int = 0, part: int = 0) -> dict:
    arg_keys = jax.random.split(jax.random.key(seed), 9)
    part_keys = jax.random.split(jax.random.fold_in(arg_keys[8], part), 9)
    return {
        "estimate": noise(part_keys[0], (PATCH, PATCHES, PATCH), 1.0, 6.0, ((0, 16),), jnp.float32),
        "observed": noise(part_keys[1], (EXPOSURES, PATCH, PATCH), 2.0, 12.0, ((0, 16),)),
        "pixel_mask": set_ends((jax.random.randint(part_keys[2], (EXPOSURES, PATCH, PATCH), 0, 10) < 9).astype(jnp.int32), jax.random.fold_in(part_keys[2], 1), 0, 1),
        "blur_mix": jnp.clip(0.2 + 0.8 * jax.random.uniform(part_keys[3], (EXPOSURES, BASES, TILES, TILES), jnp.float32) ** shard_levels(part_keys[3], (EXPOSURES, BASES, TILES, TILES), ((0, 16),), -0.2, 0.2), 0.2, 1.0),
        "dithers": draw_dithers(jax.random.fold_in(jax.random.fold_in(arg_keys[8], part), 71), part),
        "patch_of": set_ends(jax.random.randint(part_keys[5], (EXPOSURES,), 0, PATCHES), jax.random.fold_in(part_keys[5], 1), 0, PATCHES - 1).astype(jnp.int32),
        "column_taps": jnp.clip(jax.random.uniform(arg_keys[6], (BASES, TAPS), jnp.float32, 0.0, 0.119628906), 0.0, 0.119628906).astype(jnp.bfloat16),
        "row_taps": jnp.clip(jax.random.uniform(arg_keys[7], (BASES, TAPS), jnp.float32, 0.0, 0.119628906), 0.0, 0.119628906).astype(jnp.bfloat16),
    }


def band_stack(tap_values, extent, col_offset):
    half_width = tap_values.shape[1] // 2
    source = lax.broadcasted_iota(jnp.int32, (extent, extent), 0)
    target = lax.broadcasted_iota(jnp.int32, (extent, extent), 1)
    offset = source - target - col_offset + half_width
    inside = (source - col_offset >= 0) & (source - col_offset < extent)
    running = jnp.zeros((tap_values.shape[0], extent, extent), jnp.float32)
    for tap_index in range(tap_values.shape[1]):
        matches = ((offset == tap_index) & inside).astype(jnp.float32)
        running = running + tap_values[:, tap_index].astype(jnp.float32)[:, None, None] * matches[None]
    return running.astype(jnp.bfloat16)


def exposure_back(rowed, frame_data, mask_frame, blur_weights, row_shift, column_band):
    extent = frame_data.shape[0]
    basis_count = blur_weights.shape[0]
    tile_count = blur_weights.shape[1]
    tile_side = extent // tile_count
    padded = jnp.pad(rowed, ((DMAX, DMAX), (0, 0)))
    shifted = lax.dynamic_slice_in_dim(padded, DMAX + row_shift, extent, 0).reshape(extent, basis_count, extent)
    blurred = jnp.einsum("kba,bkc->kac", column_band.astype(jnp.float32), shifted.astype(jnp.float32))
    mix_full = jnp.broadcast_to(blur_weights[:, :, None, :, None], (basis_count, tile_count, tile_side, tile_count, tile_side)).reshape(basis_count, extent, extent)
    model_image = jnp.sum(mix_full * blurred, axis=0)
    residual = mask_frame.astype(jnp.float32) * (model_image - frame_data.astype(jnp.float32))
    weighted = (mix_full * residual[None]).astype(jnp.bfloat16)
    backed = jnp.einsum("kab,kbc->akc", column_band.astype(jnp.float32), weighted.astype(jnp.float32))
    backed = backed.astype(jnp.bfloat16).reshape(extent, basis_count * extent)
    return jnp.pad(backed, ((DMAX, DMAX), (0, 0)))


def back_rows(padded_back, back_stack, row_shift, patch_index, patch_count, first_row, row_count):
    picked = lax.dynamic_slice_in_dim(padded_back, first_row + DMAX - row_shift, row_count, 0)
    result = jnp.dot(picked, back_stack, preferred_element_type=jnp.float32)
    selector = lax.broadcasted_iota(jnp.int32, (1, patch_count, 1), 1) == patch_index
    return jnp.where(selector, result[:, None, :], jnp.zeros((), jnp.float32))


def reference(estimate, observed, pixel_mask, blur_mix, dithers, patch_of, column_taps, row_taps):
    extent = estimate.shape[0]
    patch_count = estimate.shape[1]
    estimate_low = estimate.astype(jnp.bfloat16)
    column_band = band_stack(column_taps, extent, 0)

    def one_exposure(running, packed):
        frame_data, mask_frame, blur_weights, shifts, patch_index = packed
        row_band = band_stack(row_taps, extent, shifts[1])
        forward_stack = jnp.transpose(row_band, (1, 0, 2)).reshape(extent, -1)
        back_stack = jnp.transpose(row_band, (0, 2, 1)).reshape(-1, extent)
        chosen = lax.dynamic_index_in_dim(estimate_low, patch_index, 1, keepdims=False)
        rowed = jnp.dot(chosen, forward_stack, preferred_element_type=jnp.float32).astype(jnp.bfloat16)
        padded_back = exposure_back(rowed, frame_data, mask_frame, blur_weights, shifts[0], column_band)
        term = back_rows(padded_back, back_stack, shifts[0], patch_index, patch_count, 0, extent)
        return running + term, None

    start_value = jnp.zeros((extent, patch_count, extent), jnp.float32)
    gradient, unused = lax.scan(one_exposure, start_value, (observed, pixel_mask, blur_mix, dithers, patch_of))
    return gradient
```

```python
import functools

import jax
import jax.numpy as jnp
from jax import lax
from jax.experimental import pallas as pl
from jax.experimental.pallas import tpu as pltpu
from jax.sharding import PartitionSpec as P

BLOCK = 128
EDGE = 16
F32 = jnp.float32
BF16 = jnp.bfloat16


def dot(a, b):
    return jnp.dot(a, b, preferred_element_type=F32)


def build_bands(taps_ref, plain_ref, flipped_ref):
    taps = taps_ref[...].astype(F32)
    bases, width = taps.shape
    half = width // 2
    extent = plain_ref.shape[1]
    blocks = extent // BLOCK
    zero = jnp.zeros((extent, extent), plain_ref.dtype)
    for k in range(bases):
        plain_ref[k] = zero
        flipped_ref[k] = zero

    for first, rows, shift in ((0, BLOCK, 0), (0, EDGE, -1), (BLOCK - EDGE, EDGE, 1)):
        shape = (rows, BLOCK)
        offset = (
            lax.broadcasted_iota(jnp.int32, shape, 0)
            + first
            - lax.broadcasted_iota(jnp.int32, shape, 1)
            - shift * BLOCK
            + half
        )
        plain = [jnp.zeros(shape, F32) for _ in range(bases)]
        flipped = [jnp.zeros(shape, F32) for _ in range(bases)]
        for t in range(width):
            match = offset == t
            for k in range(bases):
                plain[k] = jnp.where(match, taps[k : k + 1, t : t + 1], plain[k])
                other = width - 1 - t
                flipped[k] = jnp.where(match, taps[k : k + 1, other : other + 1], flipped[k])
        for k in range(bases):
            plain_block = plain[k].astype(BF16)
            flipped_block = flipped[k].astype(BF16)
            for block in range(blocks):
                if 0 <= block + shift < blocks:
                    at = (
                        k,
                        pl.ds(block * BLOCK + first, rows),
                        pl.ds((block + shift) * BLOCK, BLOCK),
                    )
                    plain_ref[at] = plain_block
                    flipped_ref[at] = flipped_block


def spread_mix(mix_ref, spread_ref):
    _, bases, tiles, _ = mix_ref.shape
    extent = spread_ref.shape[2]
    lane_tile = lax.broadcasted_iota(jnp.int32, (tiles, extent), 1) // (extent // tiles)
    for k in range(bases):
        weights = mix_ref[0, k]
        spread = jnp.zeros((tiles, extent), F32)
        for tile in range(tiles):
            spread = jnp.where(lane_tile == tile, weights[:, tile : tile + 1], spread)
        spread_ref[k] = spread


def mix_full(spread_ref, k):
    tiles, extent = spread_ref.shape[1:]
    weights = spread_ref[k]
    return jnp.broadcast_to(weights[:, None, :], (tiles, extent // tiles, extent)).reshape(
        extent, extent
    )


def one_hot(extent, shift):
    row = lax.broadcasted_iota(jnp.int32, (extent, extent), 0)
    column = lax.broadcasted_iota(jnp.int32, (extent, extent), 1)
    return jnp.where(column == row + shift, 1.0, 0.0).astype(BF16)


def exposure_term(
    chosen, shifts, observed_ref, mask_ref, spread_ref, bands, rowed_ref, model_ref, total_ref
):
    row_band, row_flip, column_band, column_flip = bands
    bases, extent, _ = row_band.shape
    row_shift, column_shift = shifts
    moved = dot(one_hot(extent, row_shift), chosen).astype(BF16)
    moved = dot(moved, one_hot(extent, -column_shift)).astype(BF16)
    rowed_ref[...] = moved
    model_ref[...] = jnp.zeros_like(model_ref)

    def forward(k, _):
        rowed = dot(rowed_ref[...], row_band[k]).astype(BF16)
        model_ref[...] += mix_full(spread_ref, k) * dot(column_flip[k], rowed)
        return 0

    lax.fori_loop(0, bases, forward, 0)
    model_ref[...] = mask_ref[0].astype(F32) * (model_ref[...] - observed_ref[0].astype(F32))
    total_ref[...] = jnp.zeros_like(total_ref)

    def backward(k, _):
        weighted = (mix_full(spread_ref, k) * model_ref[...]).astype(BF16)
        backed = dot(column_band[k], weighted).astype(BF16)
        total_ref[...] += dot(backed, row_flip[k])
        return 0

    lax.fori_loop(0, bases, backward, 0)
    back = dot(one_hot(extent, -row_shift), total_ref[...].astype(BF16)).astype(BF16)
    return dot(back, one_hot(extent, column_shift))


def local_kernel(
    dithers, patch_of, estimate, observed, mask, mix, column_taps, row_taps, term,
    row_band, row_flip, column_band, column_flip, spread, rowed, model, total,
):
    build_bands(row_taps, row_band, row_flip)
    build_bands(column_taps, column_band, column_flip)
    spread_mix(mix, spread)
    patch = patch_of[0]
    result = exposure_term(
        estimate[patch], (dithers[0, 0], dithers[0, 1]), observed, mask, spread,
        (row_band, row_flip, column_band, column_flip), rowed, model, total,
    )
    for q in range(term.shape[0]):
        term[q] = jnp.where(patch == q, result, 0.0)


def work_shapes(bases, tiles, extent):
    return [pltpu.VMEM((bases, extent, extent), BF16) for _ in range(4)] + [
        pltpu.VMEM((bases, tiles, extent), F32),
        pltpu.VMEM((extent, extent), BF16),
        pltpu.VMEM((extent, extent), F32),
        pltpu.VMEM((extent, extent), F32),
    ]


def per_device(estimate, observed, pixel_mask, blur_mix, dithers, patch_of, column_taps, row_taps):
    extent = observed.shape[1]
    patches = estimate.shape[1]
    bases, tiles = blur_mix.shape[1:3]
    vmem = pl.BlockSpec(memory_space=pltpu.VMEM)
    smem = pl.BlockSpec(memory_space=pltpu.SMEM)
    low = jnp.transpose(estimate.astype(BF16), (1, 0, 2))
    gathered = lax.all_gather(low, "exp", axis=1, tiled=True)
    term = pl.pallas_call(
        local_kernel,
        out_shape=jax.ShapeDtypeStruct((patches, extent, extent), F32),
        in_specs=[smem, smem] + [vmem] * 6,
        out_specs=vmem,
        scratch_shapes=work_shapes(bases, tiles, extent),
        compiler_params=pltpu.CompilerParams(vmem_limit_bytes=56 * 2**20),
    )(dithers, patch_of, gathered, observed, pixel_mask, blur_mix, column_taps, row_taps)
    mine = lax.psum_scatter(term, "exp", scatter_dimension=1, tiled=True)
    return jnp.transpose(mine, (1, 0, 2))


def solution(mesh):
    in_specs = (
        P("exp", "groups", None),
        P(("groups", "exp"), None, None),
        P(("groups", "exp"), None, None),
        P(("groups", "exp"), None, None, None),
        P(("groups", "exp"), None),
        P(("groups", "exp")),
        P(),
        P(),
    )
    return jax.shard_map(
        per_device,
        mesh=mesh,
        in_specs=in_specs,
        out_specs=P("exp", "groups", None),
        check_vma=False,
    )
```

```python
import functools

import jax
import jax.numpy as jnp
from jax import lax
from jax.experimental import pallas as pl
from jax.experimental.pallas import tpu as pltpu
from jax.sharding import PartitionSpec as P

BLOCK = 128
EDGE = 16
F32 = jnp.float32
BF16 = jnp.bfloat16


def dot(a, b):
    return jnp.dot(a, b, preferred_element_type=F32)


def build_bands(taps_ref, plain_ref, flipped_ref, shift, place):
    taps = taps_ref[...].astype(F32)
    bases, width = taps.shape
    half = width // 2
    extent = plain_ref.shape[1]
    blocks = extent // BLOCK
    zero = jnp.zeros((extent, extent), plain_ref.dtype)
    for k in range(bases):
        plain_ref[k] = zero
        flipped_ref[k] = zero

    for first, rows, aside in ((0, BLOCK, 0), (0, EDGE, -1), (BLOCK - EDGE, EDGE, 1)):
        shape = (rows, BLOCK)
        row = lax.broadcasted_iota(jnp.int32, shape, 0) + first
        column = lax.broadcasted_iota(jnp.int32, shape, 1) + aside * BLOCK
        ahead = row - column + (half - shift)
        behind = column - row + (half - shift)
        plain = [jnp.zeros(shape, F32) for _ in range(bases)]
        flipped = [jnp.zeros(shape, F32) for _ in range(bases)]
        for t in range(width):
            match_ahead = ahead == t
            match_behind = behind == t
            for k in range(bases):
                tap = taps[k : k + 1, t : t + 1]
                plain[k] = jnp.where(match_ahead, tap, plain[k])
                flipped[k] = jnp.where(match_behind, tap, flipped[k])
        for block in range(blocks):
            if not 0 <= block + aside < blocks:
                continue
            source = row + (block * BLOCK - shift)
            target = column + (block * BLOCK - shift)
            row_inside = (source >= 0) & (source < extent)
            column_inside = (target >= 0) & (target < extent)
            outer_row = block in (0, blocks - 1)
            outer_column = block + aside in (0, blocks - 1)
            columns = pl.ds((block + aside) * BLOCK, BLOCK)
            for k in range(bases):
                one = jnp.where(row_inside, plain[k], 0.0) if outer_row else plain[k]
                two = jnp.where(column_inside, flipped[k], 0.0) if outer_column else flipped[k]
                one, two = one.astype(BF16), two.astype(BF16)
                flipped_ref[k, pl.ds(block * BLOCK + first, rows), columns] = two
                for piece in range(0, rows, EDGE):
                    to = place(block * BLOCK + first + piece)
                    plain_ref[k, pl.ds(to, EDGE), columns] = one[piece : piece + EDGE]


def forward_residual(estimate, patch, observed, mask, spread, row_band, column_flip, model):
    def basis(k, _):
        rowed = dot(estimate[patch], row_band[k]).astype(BF16)
        model[...] += mix_full(spread, k) * dot(column_flip[k], rowed)
        return 0

    model[...] = jnp.zeros_like(model)
    lax.fori_loop(0, row_band.shape[0], basis, 0)
    model[...] = mask[0].astype(F32) * (model[...] - observed[0].astype(F32))


def backward(first, last, make, rows, spread, row_flip, column_band, model, weighted, total):
    def basis(k, _):
        if make:
            weighted[k] = (mix_full(spread, k) * model[...]).astype(BF16)
        backed = dot(column_band[k, rows, :], weighted[k]).astype(BF16)
        total[...] += dot(backed, row_flip[k])
        return 0

    lax.fori_loop(first, last, basis, 0)


def local_kernel(
    dithers, patch_of, estimate, observed, mask, mix, column_taps, row_taps, term,
    row_band, row_flip, column_band, column_flip, spread, weighted, model, total,
):
    extent = observed.shape[1]
    build_bands(row_taps, row_band, row_flip, dithers[0, 1], lambda r: r)
    build_bands(column_taps, column_band, column_flip, dithers[0, 0], lambda r: r)
    spread_mix(mix, spread)
    patch = patch_of[0]
    forward_residual(estimate, patch, observed, mask, spread, row_band, column_flip, model)
    bases = spread.shape[0]
    total[...] = jnp.zeros_like(total)
    everything = pl.ds(0, extent)
    backward(0, bases, True, everything, spread, row_flip, column_band, model, weighted, total)
    for q in range(term.shape[0]):
        term[q] = jnp.where(patch == q, total[...], 0.0)


def fused_kernel(
    size, dithers, patch_of, estimate, observed, mask, mix, column_taps, row_taps, out,
    row_band, row_flip, column_band, column_flip, spread, weighted, model, total,
    gathered, low, from_core, to_row, from_row, to_plane, from_plane,
    z_send, z_recv, y_send, y_recv, c_send, c_recv,
    rc_send, rc_recv, ry_send, ry_recv, rz_send, rz_recv,
):
    planes = size // 4
    band, patches, _ = estimate.shape
    extent = observed.shape[1]
    bases = spread.shape[0]
    quarter = extent // 4
    me = lax.axis_index("exp")
    plane, y, core = me // 4, (me // 2) % 2, me % 2

    def index(p, yy, cc):
        return p * 4 + yy * 2 + cc

    def ahead(d):
        return lax.rem(plane + d, planes)

    def behind(d):
        return lax.rem(plane + planes - d, planes)

    other_core, other_row = index(plane, y, 1 - core), index(plane, 1 - y, core)

    def copy(source, target, send, recv, device):
        return pltpu.make_async_remote_copy(
            src_ref=source, dst_ref=target, send_sem=send, recv_sem=recv,
            device_id={"exp": device}, device_id_type=pl.DeviceIdType.MESH,
        )

    def shard(owner):
        return gathered.at[:, pl.ds(pl.multiple_of(owner * band, band), band), :]

    def rows_at(start, count):
        return pl.ds(pl.multiple_of(start, count), count)

    barrier = pltpu.get_barrier_semaphore()
    partners = [other_core, other_row] + [index(ahead(d), y, core) for d in range(1, planes)]
    for partner in partners:
        pl.semaphore_signal(
            barrier, inc=1, device_id={"exp": partner}, device_id_type=pl.DeviceIdType.MESH
        )
    mine = rows_at(me * band, band)
    for q in range(patches):
        gathered[q, mine, :] = estimate[:, q, :].astype(BF16)
    pl.semaphore_wait(barrier, len(partners))

    def z_copy(d):
        return copy(shard(me), shard(me), z_send.at[d], z_recv.at[d], index(ahead(d), y, core))

    def y_copy(d):
        held = shard(index(behind(d), y, core))
        return copy(held, held, y_send.at[d], y_recv.at[d], other_row)

    def c_copy(d, across):
        held = shard(index(behind(d), (1 - y) if across else y, core))
        slot = d * 2 + across
        return copy(held, held, c_send.at[slot], c_recv.at[slot], other_core)

    for d in range(1, planes):
        z_copy(d).start()
    y_copy(0).start()
    c_copy(0, 0).start()
    build_bands(row_taps, row_band, row_flip, dithers[0, 1], lambda r: r)
    for d in range(1, planes):
        z_copy(d).wait_recv()
        y_copy(d).start()
        c_copy(d, 0).start()

    def place(r):
        owner, within = r // band, r % band
        p, yy, cc = owner // 4, (owner // 2) % 2, owner % 2
        return ((yy * 2 + cc) * planes + p) * band + within

    build_bands(column_taps, column_band, column_flip, dithers[0, 0], place)
    spread_mix(mix, spread)
    for d in range(planes):
        y_copy(d).wait_recv()
        c_copy(d, 1).start()
    for d in range(planes):
        for across in (0, 1):
            c_copy(d, across).wait_recv()

    patch = patch_of[0]
    forward_residual(gathered, patch, observed, mask, spread, row_band, column_flip, model)

    def share(yy, cc):
        return low.at[:, rows_at((yy * 2 + cc) * quarter, quarter), :]

    def finish(yy):
        half = rows_at(yy * 2 * quarter, 2 * quarter)
        for q in range(patches):
            low[q, half, :] = jnp.where(patch == q, total[...], 0.0).astype(BF16)

    def rc_copy(slot, yy):
        return copy(
            share(yy, 1 - core), from_core.at[slot], rc_send.at[slot], rc_recv.at[slot], other_core
        )

    def piece(ref, p):
        return ref.at[:, rows_at(p * band, band), :]

    def ry_copy(d):
        p = ahead(d)
        return copy(piece(to_row, p), piece(from_row, p), ry_send.at[d], ry_recv.at[d], other_row)

    def rz_copy(d):
        return copy(
            to_plane.at[d], from_plane.at[d], rz_send.at[d], rz_recv.at[d],
            index(ahead(d), y, core),
        )

    def back(first, last, make, yy):
        half = rows_at(yy * 2 * quarter, 2 * quarter)
        backward(first, last, make, half, spread, row_flip, column_band, model, weighted, total)

    order = list(range(1, planes)) + [0]
    total[...] = jnp.zeros_like(total)
    back(0, bases, True, 1 - y)
    finish(1 - y)
    rc_copy(0, 1 - y).start()
    total[...] = jnp.zeros_like(total)
    back(0, bases // 2, False, y)
    rc_copy(0, 1 - y).wait_recv()
    own = rows_at(((1 - y) * 2 + core) * quarter, quarter)
    for q in range(patches):
        to_row[q] = (low[q, own, :].astype(F32) + from_core[0, q].astype(F32)).astype(BF16)
    for d in order:
        ry_copy(d).start()
    back(bases // 2, bases, False, y)
    finish(y)
    rc_copy(1, y).start()
    rc_copy(1, y).wait_recv()

    def summed(d, q):
        p = ahead(d)
        rows = rows_at((y * 2 + core) * quarter + p * band, band)
        arrived = rows_at(p * band, band)
        return (
            low[q, rows, :].astype(F32)
            + from_core[1, q, arrived, :].astype(F32)
            + from_row[q, arrived, :].astype(F32)
        )

    for d in range(1, planes):
        ry_copy(d).wait_recv()
        for q in range(patches):
            to_plane[d, q] = summed(d, q).astype(BF16)
        rz_copy(d).start()
    ry_copy(0).wait_recv()
    final = [summed(0, q) for q in range(patches)]
    for d in range(1, planes):
        rz_copy(d).wait_recv()
        for q in range(patches):
            final[q] = final[q] + from_plane[d, q].astype(F32)
    for q in range(patches):
        out[:, q, :] = final[q]

    for d in range(planes):
        if d > 0:
            z_copy(d).wait_send()
            rz_copy(d).wait_send()
        y_copy(d).wait_send()
        c_copy(d, 0).wait_send()
        c_copy(d, 1).wait_send()
        ry_copy(d).wait_send()
    rc_copy(0, 1 - y).wait_send()
    rc_copy(1, y).wait_send()


def work_shapes(bases, tiles, extent, total_rows):
    return [pltpu.VMEM((bases, extent, extent), BF16) for _ in range(4)] + [
        pltpu.VMEM((bases, tiles, extent), F32),
        pltpu.VMEM((bases, extent, extent), BF16),
        pltpu.VMEM((extent, extent), F32),
        pltpu.VMEM((total_rows, extent), F32),
    ]


def per_device(
    size, estimate, observed, pixel_mask, blur_mix, dithers, patch_of, column_taps, row_taps
):
    extent = observed.shape[1]
    band, patches, _ = estimate.shape
    bases, tiles = blur_mix.shape[1:3]
    vmem = pl.BlockSpec(memory_space=pltpu.VMEM)
    smem = pl.BlockSpec(memory_space=pltpu.SMEM)
    in_specs = [smem, smem] + [vmem] * 6
    limit = 56 * 2**20
    if size % 4 == 0 and size >= 8 and band % EDGE == 0:
        planes, quarter = size // 4, extent // 4
        sems = [planes, planes, planes, planes, 2 * planes, 2 * planes, 2, 2] + [planes] * 4
        return pl.pallas_call(
            functools.partial(fused_kernel, size),
            out_shape=jax.ShapeDtypeStruct(estimate.shape, F32),
            in_specs=in_specs,
            out_specs=vmem,
            scratch_shapes=work_shapes(bases, tiles, extent, extent // 2)
            + [
                pltpu.VMEM((patches, extent, extent), BF16),
                pltpu.VMEM((patches, extent, extent), BF16),
                pltpu.VMEM((2, patches, quarter, extent), BF16),
                pltpu.VMEM((patches, quarter, extent), BF16),
                pltpu.VMEM((patches, quarter, extent), BF16),
                pltpu.VMEM((planes, patches, band, extent), BF16),
                pltpu.VMEM((planes, patches, band, extent), BF16),
            ]
            + [pltpu.SemaphoreType.DMA((count,)) for count in sems],
            compiler_params=pltpu.CompilerParams(
                collective_id=0, has_side_effects=True, vmem_limit_bytes=limit
            ),
        )(dithers, patch_of, estimate, observed, pixel_mask, blur_mix, column_taps, row_taps)

    low = jnp.transpose(estimate.astype(BF16), (1, 0, 2))
    gathered = lax.all_gather(low, "exp", axis=1, tiled=True)
    term = pl.pallas_call(
        local_kernel,
        out_shape=jax.ShapeDtypeStruct((patches, extent, extent), F32),
        in_specs=in_specs,
        out_specs=vmem,
        scratch_shapes=work_shapes(bases, tiles, extent, extent),
        compiler_params=pltpu.CompilerParams(vmem_limit_bytes=limit),
    )(dithers, patch_of, gathered, observed, pixel_mask, blur_mix, column_taps, row_taps)
    mine = lax.psum_scatter(term, "exp", scatter_dimension=1, tiled=True)
    return jnp.transpose(mine, (1, 0, 2))


def spread_mix(mix_ref, spread_ref):
    _, bases, tiles, _ = mix_ref.shape
    extent = spread_ref.shape[2]
    lane_tile = lax.broadcasted_iota(jnp.int32, (tiles, extent), 1) // (extent // tiles)
    for k in range(bases):
        weights = mix_ref[0, k]
        spread = jnp.zeros((tiles, extent), F32)
        for tile in range(tiles):
            spread = jnp.where(lane_tile == tile, weights[:, tile : tile + 1], spread)
        spread_ref[k] = spread


def mix_full(spread_ref, k):
    tiles, extent = spread_ref.shape[1:]
    weights = spread_ref[k]
    return jnp.broadcast_to(weights[:, None, :], (tiles, extent // tiles, extent)).reshape(
        extent, extent
    )


def solution(mesh):
    in_specs = (
        P("exp", "groups", None),
        P(("groups", "exp"), None, None),
        P(("groups", "exp"), None, None),
        P(("groups", "exp"), None, None, None),
        P(("groups", "exp"), None),
        P(("groups", "exp")),
        P(),
        P(),
    )
    return jax.shard_map(
        functools.partial(per_device, mesh.shape["exp"]),
        mesh=mesh,
        in_specs=in_specs,
        out_specs=P("exp", "groups", None),
        check_vma=False,
    )
```

```python
import functools

import jax
import jax.numpy as jnp
from jax import lax
from jax.experimental import pallas as pl
from jax.experimental.pallas import tpu as pltpu
from jax.sharding import PartitionSpec as P

BLOCK = 128
EDGE = 16
F32 = jnp.float32
BF16 = jnp.bfloat16


def dot(a, b):
    return jnp.dot(a, b, preferred_element_type=F32)


def build_bands(taps_ref, plain_ref, flipped_ref, shift, place):
    taps = taps_ref[...].astype(F32)
    bases, width = taps.shape
    half = width // 2
    extent = plain_ref.shape[1]
    blocks = extent // BLOCK
    zero = jnp.zeros((extent, extent), plain_ref.dtype)
    for k in range(bases):
        plain_ref[k] = zero
        flipped_ref[k] = zero

    for first, rows, aside in ((0, BLOCK, 0), (0, EDGE, -1), (BLOCK - EDGE, EDGE, 1)):
        shape = (rows, BLOCK)
        row = lax.broadcasted_iota(jnp.int32, shape, 0) + first
        column = lax.broadcasted_iota(jnp.int32, shape, 1) + aside * BLOCK
        ahead = row - column + (half - shift)
        behind = column - row + (half - shift)
        plain = [jnp.zeros(shape, F32) for _ in range(bases)]
        flipped = [jnp.zeros(shape, F32) for _ in range(bases)]
        for t in range(width):
            match_ahead = ahead == t
            match_behind = behind == t
            for k in range(bases):
                tap = taps[k : k + 1, t : t + 1]
                plain[k] = jnp.where(match_ahead, tap, plain[k])
                flipped[k] = jnp.where(match_behind, tap, flipped[k])
        for block in range(blocks):
            if not 0 <= block + aside < blocks:
                continue
            source = row + (block * BLOCK - shift)
            target = column + (block * BLOCK - shift)
            row_inside = (source >= 0) & (source < extent)
            column_inside = (target >= 0) & (target < extent)
            outer_row = block in (0, blocks - 1)
            outer_column = block + aside in (0, blocks - 1)
            columns = pl.ds((block + aside) * BLOCK, BLOCK)
            for k in range(bases):
                one = jnp.where(row_inside, plain[k], 0.0) if outer_row else plain[k]
                two = jnp.where(column_inside, flipped[k], 0.0) if outer_column else flipped[k]
                one, two = one.astype(BF16), two.astype(BF16)
                flipped_ref[k, pl.ds(block * BLOCK + first, rows), columns] = two
                for piece in range(0, rows, EDGE):
                    to = place(block * BLOCK + first + piece)
                    plain_ref[k, pl.ds(to, EDGE), columns] = one[piece : piece + EDGE]


def forward_residual(observed, mask, spread, column_flip, rowed, model):
    bases = spread.shape[0]
    model[...] = mix_full(spread, 0) * dot(column_flip[0], rowed[0])

    def basis(k, _):
        model[...] += mix_full(spread, k) * dot(column_flip[k], rowed[k])
        return 0

    lax.fori_loop(1, bases, basis, 0, unroll=True)
    model[...] = mask[...].astype(F32) * (model[...] - observed[...].astype(F32))


def backward(first, last, make, rows, spread, row_flip, column_band, model, weighted, total):
    def basis(k, _):
        if make:
            weighted[k] = (mix_full(spread, k) * model[...]).astype(BF16)
        backed = dot(column_band[k, rows, :], weighted[k]).astype(BF16)
        total[...] += dot(backed, row_flip[k])
        return 0

    lax.fori_loop(first, last, basis, 0, unroll=True)


def local_kernel(
    dithers, patch_of, estimate, observed, mask, mix, column_taps, row_taps, term,
    row_band, row_flip, column_band, column_flip, spread, weighted, model, total,
):
    extent = observed.shape[1]
    build_bands(row_taps, row_band, row_flip, dithers[0, 1], lambda r: r)
    build_bands(column_taps, column_band, column_flip, dithers[0, 0], lambda r: r)
    spread_mix(mix, spread)
    patch = patch_of[0]
    bases = spread.shape[0]
    for k in range(bases):
        weighted[k] = dot(estimate[patch], row_band[k]).astype(BF16)
    forward_residual(observed.at[0], mask.at[0], spread, column_flip, weighted, model)
    total[...] = jnp.zeros_like(total)
    everything = pl.ds(0, extent)
    backward(0, bases, True, everything, spread, row_flip, column_band, model, weighted, total)
    for q in range(term.shape[0]):
        term[q] = jnp.where(patch == q, total[...], 0.0)


def fused_kernel(
    size, dithers, patch_of, estimate, observed, mask, mix, column_taps, row_taps, out,
    row_band, row_flip, column_band, column_flip, spread, weighted, model, total,
    gathered, low, from_core, to_row, from_row, to_plane, from_plane,
    z_send, z_recv, y_send, y_recv, c_send, c_recv,
    rc_send, rc_recv, ry_send, ry_recv, rz_send, rz_recv, frame, good, load_sem,
):
    planes = size // 4
    band, patches, _ = estimate.shape
    extent = observed.shape[1]
    bases = spread.shape[0]
    quarter = extent // 4
    me = lax.axis_index("exp")
    plane, y, core = me // 4, (me // 2) % 2, me % 2

    def index(p, yy, cc):
        return p * 4 + yy * 2 + cc

    def ahead(d):
        return lax.rem(plane + d, planes)

    def behind(d):
        return lax.rem(plane + planes - d, planes)

    other_core, other_row = index(plane, y, 1 - core), index(plane, 1 - y, core)

    def copy(source, target, send, recv, device):
        return pltpu.make_async_remote_copy(
            src_ref=source, dst_ref=target, send_sem=send, recv_sem=recv,
            device_id={"exp": device}, device_id_type=pl.DeviceIdType.MESH,
        )

    def shard(owner):
        return gathered.at[:, pl.ds(pl.multiple_of(owner * band, band), band), :]

    def rows_at(start, count):
        return pl.ds(pl.multiple_of(start, count), count)

    loads = [
        pltpu.make_async_copy(observed.at[0], frame, load_sem.at[0]),
        pltpu.make_async_copy(mask.at[0], good, load_sem.at[1]),
    ]
    barrier = pltpu.get_barrier_semaphore()
    partners = [other_core, other_row] + [index(ahead(d), y, core) for d in range(1, planes)]
    for partner in partners:
        pl.semaphore_signal(
            barrier, inc=1, device_id={"exp": partner}, device_id_type=pl.DeviceIdType.MESH
        )
    mine = rows_at(me * band, band)
    for q in range(patches):
        gathered[q, mine, :] = estimate[:, q, :].astype(BF16)
    pl.semaphore_wait(barrier, len(partners))

    def z_copy(d):
        return copy(shard(me), shard(me), z_send.at[d], z_recv.at[d], index(ahead(d), y, core))

    def y_copy(d):
        held = shard(index(behind(d), y, core))
        return copy(held, held, y_send.at[d], y_recv.at[d], other_row)

    def c_copy(d, across):
        held = shard(index(behind(d), (1 - y) if across else y, core))
        slot = d * 2 + across
        return copy(held, held, c_send.at[slot], c_recv.at[slot], other_core)

    y_copy(0).start()
    for d in range(1, planes):
        z_copy(d).start()
    c_copy(0, 0).start()
    for load in loads:
        load.start()
    build_bands(row_taps, row_band, row_flip, dithers[0, 1], lambda r: r)
    for d in range(1, planes):
        z_copy(d).wait_recv()
        y_copy(d).start()
        c_copy(d, 0).start()

    def place(r):
        owner, within = r // band, r % band
        p, yy, cc = owner // 4, (owner // 2) % 2, owner % 2
        return ((yy * 2 + cc) * planes + p) * band + within

    def forward_y(d):
        y_copy(d).wait_recv()
        c_copy(d, 1).start()

    def blur_rows(yy):
        starts = [p * 4 * band + yy * 2 * band for p in range(planes)]

        def of_patch(q):
            return jnp.concatenate(
                [gathered[q, rows_at(start, 2 * band), :] for start in starts], axis=0
            )

        joined = of_patch(0)
        for q in range(1, patches):
            joined = jnp.where(patch == q, of_patch(q), joined)
        for k in range(bases):
            rowed = dot(joined, row_band[k]).astype(BF16)
            for p in range(planes):
                piece_rows = rowed[p * 2 * band : (p + 1) * 2 * band]
                weighted[k, rows_at(starts[p], 2 * band), :] = piece_rows

    patch = patch_of[0]
    forward_y(0)
    build_bands(column_taps, column_band, column_flip, dithers[0, 0], place)
    spread_mix(mix, spread)
    forward_y(1)
    for d in range(planes):
        c_copy(d, 0).wait_recv()
    blur_rows(y)
    for d in range(2, planes):
        forward_y(d)
    for d in range(planes):
        c_copy(d, 1).wait_recv()
    blur_rows(1 - y)
    for load in loads:
        load.wait()
    forward_residual(frame, good, spread, column_flip, weighted, model)

    def finish(yy):
        half = rows_at(yy * 2 * quarter, 2 * quarter)
        for q in range(patches):
            low[q, half, :] = jnp.where(patch == q, total[...], 0.0).astype(BF16)

    def rc_copy(slot, d):
        yy = y if slot else 1 - y
        p = ahead(d)
        at = slot * planes + d
        rows = rows_at((yy * 2 + 1 - core) * quarter + p * band, band)
        return copy(
            low.at[:, rows, :], from_core.at[slot, :, rows_at(p * band, band), :],
            rc_send.at[at], rc_recv.at[at], other_core,
        )

    def piece(ref, p):
        return ref.at[:, rows_at(p * band, band), :]

    def ry_copy(d):
        p = ahead(d)
        return copy(piece(to_row, p), piece(from_row, p), ry_send.at[d], ry_recv.at[d], other_row)

    def rz_copy(d):
        return copy(
            to_plane.at[d], from_plane.at[d], rz_send.at[d], rz_recv.at[d],
            index(ahead(d), y, core),
        )

    def back(first, last, make, yy):
        half = rows_at(yy * 2 * quarter, 2 * quarter)
        backward(first, last, make, half, spread, row_flip, column_band, model, weighted, total)

    order = list(range(1, planes)) + [0]
    total[...] = jnp.zeros_like(total)
    back(0, bases, True, 1 - y)
    finish(1 - y)
    for d in order:
        rc_copy(0, d).start()
    total[...] = jnp.zeros_like(total)
    back(0, bases // 2, False, y)
    for d in order:
        rc_copy(0, d).wait_recv()
        p = ahead(d)
        own = rows_at(((1 - y) * 2 + core) * quarter + p * band, band)
        arrived = rows_at(p * band, band)
        for q in range(patches):
            both = low[q, own, :].astype(F32) + from_core[0, q, arrived, :].astype(F32)
            to_row[q, arrived, :] = both.astype(BF16)
        ry_copy(d).start()
    back(bases // 2, bases, False, y)
    finish(y)
    for d in order:
        rc_copy(1, d).start()

    def summed(d, q):
        p = ahead(d)
        rows = rows_at((y * 2 + core) * quarter + p * band, band)
        arrived = rows_at(p * band, band)
        return (
            low[q, rows, :].astype(F32)
            + from_core[1, q, arrived, :].astype(F32)
            + from_row[q, arrived, :].astype(F32)
        )

    for d in range(1, planes):
        rc_copy(1, d).wait_recv()
        ry_copy(d).wait_recv()
        for q in range(patches):
            to_plane[d, q] = summed(d, q).astype(BF16)
        rz_copy(d).start()
    rc_copy(1, 0).wait_recv()
    ry_copy(0).wait_recv()
    final = [summed(0, q) for q in range(patches)]
    for d in range(1, planes):
        rz_copy(d).wait_recv()
        for q in range(patches):
            final[q] = final[q] + from_plane[d, q].astype(F32)
    for q in range(patches):
        out[:, q, :] = final[q]

    for d in range(planes):
        if d > 0:
            z_copy(d).wait_send()
            rz_copy(d).wait_send()
        y_copy(d).wait_send()
        c_copy(d, 0).wait_send()
        c_copy(d, 1).wait_send()
        ry_copy(d).wait_send()
        rc_copy(0, d).wait_send()
        rc_copy(1, d).wait_send()


def work_shapes(bases, tiles, extent, total_rows):
    return [pltpu.VMEM((bases, extent, extent), BF16) for _ in range(4)] + [
        pltpu.VMEM((bases, tiles, extent), F32),
        pltpu.VMEM((bases, extent, extent), BF16),
        pltpu.VMEM((extent, extent), F32),
        pltpu.VMEM((total_rows, extent), F32),
    ]


def per_device(
    size, estimate, observed, pixel_mask, blur_mix, dithers, patch_of, column_taps, row_taps
):
    extent = observed.shape[1]
    band, patches, _ = estimate.shape
    bases, tiles = blur_mix.shape[1:3]
    vmem = pl.BlockSpec(memory_space=pltpu.VMEM)
    smem = pl.BlockSpec(memory_space=pltpu.SMEM)
    in_specs = [smem, smem] + [vmem] * 6
    limit = 56 * 2**20
    if size % 4 == 0 and size >= 8 and band % EDGE == 0:
        planes, quarter = size // 4, extent // 4
        sems = [planes, planes, planes, planes, 2 * planes, 2 * planes] + [2 * planes] * 2 + [planes] * 4
        return pl.pallas_call(
            functools.partial(fused_kernel, size),
            out_shape=jax.ShapeDtypeStruct(estimate.shape, F32),
            in_specs=[smem, smem, vmem] + [pl.BlockSpec(memory_space=pl.ANY)] * 2 + [vmem] * 3,
            out_specs=vmem,
            scratch_shapes=work_shapes(bases, tiles, extent, extent // 2)
            + [
                pltpu.VMEM((patches, extent, extent), BF16),
                pltpu.VMEM((patches, extent, extent), BF16),
                pltpu.VMEM((2, patches, quarter, extent), BF16),
                pltpu.VMEM((patches, quarter, extent), BF16),
                pltpu.VMEM((patches, quarter, extent), BF16),
                pltpu.VMEM((planes, patches, band, extent), BF16),
                pltpu.VMEM((planes, patches, band, extent), BF16),
            ]
            + [pltpu.SemaphoreType.DMA((count,)) for count in sems]
            + [
                pltpu.VMEM((extent, extent), observed.dtype),
                pltpu.VMEM((extent, extent), pixel_mask.dtype),
                pltpu.SemaphoreType.DMA((2,)),
            ],
            compiler_params=pltpu.CompilerParams(
                collective_id=0, has_side_effects=True, vmem_limit_bytes=limit
            ),
        )(dithers, patch_of, estimate, observed, pixel_mask, blur_mix, column_taps, row_taps)

    low = jnp.transpose(estimate.astype(BF16), (1, 0, 2))
    gathered = lax.all_gather(low, "exp", axis=1, tiled=True)
    term = pl.pallas_call(
        local_kernel,
        out_shape=jax.ShapeDtypeStruct((patches, extent, extent), F32),
        in_specs=in_specs,
        out_specs=vmem,
        scratch_shapes=work_shapes(bases, tiles, extent, extent),
        compiler_params=pltpu.CompilerParams(vmem_limit_bytes=limit),
    )(dithers, patch_of, gathered, observed, pixel_mask, blur_mix, column_taps, row_taps)
    mine = lax.psum_scatter(term, "exp", scatter_dimension=1, tiled=True)
    return jnp.transpose(mine, (1, 0, 2))


def spread_mix(mix_ref, spread_ref):
    _, bases, tiles, _ = mix_ref.shape
    extent = spread_ref.shape[2]
    lane_tile = lax.broadcasted_iota(jnp.int32, (tiles, extent), 1) // (extent // tiles)
    for k in range(bases):
        weights = mix_ref[0, k]
        spread = jnp.zeros((tiles, extent), F32)
        for tile in range(tiles):
            spread = jnp.where(lane_tile == tile, weights[:, tile : tile + 1], spread)
        spread_ref[k] = spread


def mix_full(spread_ref, k):
    tiles, extent = spread_ref.shape[1:]
    weights = spread_ref[k]
    return jnp.broadcast_to(weights[:, None, :], (tiles, extent // tiles, extent)).reshape(
        extent, extent
    )


def solution(mesh):
    in_specs = (
        P("exp", "groups", None),
        P(("groups", "exp"), None, None),
        P(("groups", "exp"), None, None),
        P(("groups", "exp"), None, None, None),
        P(("groups", "exp"), None),
        P(("groups", "exp")),
        P(),
        P(),
    )
    return jax.shard_map(
        functools.partial(per_device, mesh.shape["exp"]),
        mesh=mesh,
        in_specs=in_specs,
        out_specs=P("exp", "groups", None),
        check_vma=False,
    )
```

```python
import functools

import jax
import jax.numpy as jnp
from jax import lax
from jax.experimental import pallas as pl
from jax.experimental.pallas import tpu as pltpu
from jax.sharding import PartitionSpec as P

BLOCK = 128
EDGE = 16
F32 = jnp.float32
BF16 = jnp.bfloat16


def dot(a, b):
    return jnp.dot(a, b, preferred_element_type=F32)


def build_bands(taps_ref, plain_ref, flipped_ref, shift):
    taps = taps_ref[...].astype(F32)
    bases, width = taps.shape
    half = width // 2
    extent = plain_ref.shape[1]
    blocks = extent // BLOCK
    zero = jnp.zeros((extent, extent), plain_ref.dtype)
    for k in range(bases):
        plain_ref[k] = zero
        flipped_ref[k] = zero

    for first, rows, aside in ((0, BLOCK, 0), (0, EDGE, -1), (BLOCK - EDGE, EDGE, 1)):
        shape = (rows, BLOCK)
        row = lax.broadcasted_iota(jnp.int32, shape, 0) + first
        column = lax.broadcasted_iota(jnp.int32, shape, 1) + aside * BLOCK
        ahead = row - column + (half - shift)
        behind = column - row + (half - shift)
        plain = [jnp.zeros(shape, F32) for _ in range(bases)]
        flipped = [jnp.zeros(shape, F32) for _ in range(bases)]
        for t in range(width):
            match_ahead = ahead == t
            match_behind = behind == t
            for k in range(bases):
                tap = taps[k : k + 1, t : t + 1]
                plain[k] = jnp.where(match_ahead, tap, plain[k])
                flipped[k] = jnp.where(match_behind, tap, flipped[k])
        for block in range(blocks):
            if not 0 <= block + aside < blocks:
                continue
            source = row + (block * BLOCK - shift)
            target = column + (block * BLOCK - shift)
            row_inside = (source >= 0) & (source < extent)
            column_inside = (target >= 0) & (target < extent)
            outer_row = block in (0, blocks - 1)
            outer_column = block + aside in (0, blocks - 1)
            columns = pl.ds((block + aside) * BLOCK, BLOCK)
            for k in range(bases):
                one = jnp.where(row_inside, plain[k], 0.0) if outer_row else plain[k]
                two = jnp.where(column_inside, flipped[k], 0.0) if outer_column else flipped[k]
                one, two = one.astype(BF16), two.astype(BF16)
                stored = pl.ds(block * BLOCK + first, rows)
                plain_ref[k, stored, columns] = one
                flipped_ref[k, stored, columns] = two


def forward_residual(observed, mask, spread, column_flip, rowed, model):
    bases = spread.shape[0]
    model[...] = mix_full(spread, 0) * dot(column_flip[0], rowed[0])

    def basis(k, _):
        model[...] += mix_full(spread, k) * dot(column_flip[k], rowed[k])
        return 0

    lax.fori_loop(1, bases, basis, 0, unroll=True)
    model[...] = mask[...].astype(F32) * (model[...] - observed[...].astype(F32))


def backward(first, last, make, rows, spread, row_flip, column_band, model, weighted, total):
    def basis(k, _):
        if make:
            weighted[k] = (mix_full(spread, k) * model[...]).astype(BF16)
        backed = dot(column_band[k, rows, :], weighted[k]).astype(BF16)
        total[...] += dot(backed, row_flip[k])
        return 0

    lax.fori_loop(first, last, basis, 0, unroll=True)


def local_kernel(
    dithers, patch_of, estimate, observed, mask, mix, column_taps, row_taps, term,
    row_band, row_flip, column_band, column_flip, spread, weighted, model, total,
):
    extent = observed.shape[1]
    build_bands(row_taps, row_band, row_flip, dithers[0, 1])
    build_bands(column_taps, column_band, column_flip, dithers[0, 0])
    spread_mix(mix, spread)
    patch = patch_of[0]
    bases = spread.shape[0]
    for k in range(bases):
        weighted[k] = dot(estimate[patch], row_band[k]).astype(BF16)
    forward_residual(observed.at[0], mask.at[0], spread, column_flip, weighted, model)
    total[...] = jnp.zeros_like(total)
    everything = pl.ds(0, extent)
    backward(0, bases, True, everything, spread, row_flip, column_band, model, weighted, total)
    for q in range(term.shape[0]):
        term[q] = jnp.where(patch == q, total[...], 0.0)


def fused_kernel(
    size, dithers, patch_of, estimate, observed, mask, mix, column_taps, row_taps, out,
    row_band, row_flip, column_band, column_flip, spread, weighted, model, total,
    gathered, low, from_core, to_row, from_row, to_plane, from_plane,
    z_send, z_recv, y_send, y_recv, c_send, c_recv,
    rc_send, rc_recv, ry_send, ry_recv, rz_send, rz_recv, frame, good, load_sem,
):
    planes = size // 4
    band, patches, _ = estimate.shape
    extent = observed.shape[1]
    bases = spread.shape[0]
    me = lax.axis_index("exp")
    plane, y, core = me // 4, (me // 2) % 2, me % 2

    def index(p, yy, cc):
        return p * 4 + yy * 2 + cc

    def mirror(x):
        p, bit = 0, 1
        while bit < planes:
            p = p + ((plane // bit + x // bit) % 2) * bit
            bit *= 2
        return p

    other_core, other_row = index(plane, y, 1 - core), index(plane, 1 - y, core)

    def copy(source, target, send, recv, device):
        return pltpu.make_async_remote_copy(
            src_ref=source, dst_ref=target, send_sem=send, recv_sem=recv,
            device_id={"exp": device}, device_id_type=pl.DeviceIdType.MESH,
        )

    def shard(owner):
        return gathered.at[:, pl.ds(pl.multiple_of(owner * band, band), band), :]

    def rows_at(start, count):
        return pl.ds(pl.multiple_of(start, count), count)

    near, far = list(range(planes // 2)), list(range(planes // 2, planes))
    loads = [
        pltpu.make_async_copy(observed.at[0], frame, load_sem.at[0]),
        pltpu.make_async_copy(mask.at[0], good, load_sem.at[1]),
    ]
    barrier = pltpu.get_barrier_semaphore()
    partners = [other_core, other_row] + [index(mirror(d), y, core) for d in range(1, planes)]
    for partner in partners:
        pl.semaphore_signal(
            barrier, inc=1, device_id={"exp": partner}, device_id_type=pl.DeviceIdType.MESH
        )
    mine = rows_at(me * band, band)
    for q in range(patches):
        gathered[q, mine, :] = estimate[:, q, :].astype(BF16)
    pl.semaphore_wait(barrier, len(partners))

    def z_copy(d):
        return copy(shard(me), shard(me), z_send.at[d], z_recv.at[d], index(mirror(d), y, core))

    def y_copy(d):
        held = shard(index(mirror(d), y, core))
        return copy(held, held, y_send.at[d], y_recv.at[d], other_row)

    def c_copy(d, across):
        held = shard(index(mirror(d), (1 - y) if across else y, core))
        slot = d * 2 + across
        return copy(held, held, c_send.at[slot], c_recv.at[slot], other_core)

    y_copy(0).start()
    for d in far + near[1:]:
        z_copy(d).start()
    c_copy(0, 0).start()
    for load in loads:
        load.start()
    build_bands(row_taps, row_band, row_flip, dithers[0, 1])
    for d in range(1, planes):
        z_copy(d).wait_recv()
        y_copy(d).start()
        c_copy(d, 0).start()

    def forward_y(d):
        y_copy(d).wait_recv()
        c_copy(d, 1).start()

    def blur_rows(yy):
        starts = [p * 4 * band + yy * 2 * band for p in range(planes)]

        def of_patch(q):
            return jnp.concatenate(
                [gathered[q, rows_at(start, 2 * band), :] for start in starts], axis=0
            )

        joined = of_patch(0)
        for q in range(1, patches):
            joined = jnp.where(patch == q, of_patch(q), joined)
        for k in range(bases):
            rowed = dot(joined, row_band[k]).astype(BF16)
            for p in range(planes):
                piece_rows = rowed[p * 2 * band : (p + 1) * 2 * band]
                weighted[k, rows_at(starts[p], 2 * band), :] = piece_rows

    patch = patch_of[0]
    forward_y(0)
    build_bands(column_taps, column_band, column_flip, dithers[0, 0])
    spread_mix(mix, spread)
    forward_y(1)
    for d in range(planes):
        c_copy(d, 0).wait_recv()
    blur_rows(y)
    for d in range(2, planes):
        forward_y(d)
    for d in range(planes):
        c_copy(d, 1).wait_recv()
    for load in loads:
        load.wait()
    blur_rows(1 - y)
    forward_residual(frame, good, spread, column_flip, weighted, model)

    def owned(d, yy, cc):
        return rows_at(index(mirror(d), yy, cc) * band, band)

    def half_rows(planes_of):
        lowest = mirror(planes_of[0]) // len(planes_of) * len(planes_of)
        return rows_at(lowest * 4 * band, extent // 2)

    def rc_copy(d, across):
        slot = d * 2 + across
        rows = owned(d, (1 - y) if across else y, 1 - core)
        return copy(
            low.at[:, rows, :], from_core.at[slot], rc_send.at[slot], rc_recv.at[slot], other_core
        )

    def ry_copy(d):
        return copy(to_row.at[d], from_row.at[d], ry_send.at[d], ry_recv.at[d], other_row)

    def rz_copy(d):
        return copy(
            to_plane.at[d], from_plane.at[d], rz_send.at[d], rz_recv.at[d],
            index(mirror(d), y, core),
        )

    def back(first, last, make, planes_of):
        half = half_rows(planes_of)
        backward(first, last, make, half, spread, row_flip, column_band, model, weighted, total)

    def to_core(planes_of):
        half = half_rows(planes_of)
        for q in range(patches):
            low[q, half, :] = jnp.where(patch == q, total[...], 0.0).astype(BF16)
        for across in (1, 0):
            for d in planes_of:
                rc_copy(d, across).start()

    def core_sum(d, across, q):
        rows = owned(d, (1 - y) if across else y, core)
        return low[q, rows, :].astype(F32) + from_core[d * 2 + across, q].astype(F32)

    def to_other_row(planes_of):
        for d in planes_of:
            rc_copy(d, 1).wait_recv()
            for q in range(patches):
                to_row[d, q] = core_sum(d, 1, q).astype(BF16)
            ry_copy(d).start()

    def row_sum(d):
        rc_copy(d, 0).wait_recv()
        ry_copy(d).wait_recv()
        return [core_sum(d, 0, q) + from_row[d, q].astype(F32) for q in range(patches)]

    def to_other_plane(d):
        sums = row_sum(d)
        for q in range(patches):
            to_plane[d, q] = sums[q].astype(BF16)
        rz_copy(d).start()

    near_last = near[1:] + near[:1]
    total[...] = jnp.zeros_like(total)
    back(0, bases, True, far)
    to_core(far)
    total[...] = jnp.zeros_like(total)
    back(0, bases // 2, False, near)
    to_other_row(far)
    back(bases // 2, bases, False, near)
    to_core(near_last)
    to_other_plane(far[0])
    to_other_row(near_last)
    for d in far[1:] + near[1:]:
        to_other_plane(d)
    final = row_sum(0)
    for d in near[1:] + far:
        rz_copy(d).wait_recv()
        for q in range(patches):
            final[q] = final[q] + from_plane[d, q].astype(F32)
    for q in range(patches):
        out[:, q, :] = final[q]

    for d in range(planes):
        if d > 0:
            z_copy(d).wait_send()
            rz_copy(d).wait_send()
        y_copy(d).wait_send()
        c_copy(d, 0).wait_send()
        c_copy(d, 1).wait_send()
        ry_copy(d).wait_send()
        rc_copy(d, 0).wait_send()
        rc_copy(d, 1).wait_send()


def work_shapes(bases, tiles, extent, total_rows):
    return [pltpu.VMEM((bases, extent, extent), BF16) for _ in range(4)] + [
        pltpu.VMEM((bases, tiles, extent), F32),
        pltpu.VMEM((bases, extent, extent), BF16),
        pltpu.VMEM((extent, extent), F32),
        pltpu.VMEM((total_rows, extent), F32),
    ]


def per_device(
    size, estimate, observed, pixel_mask, blur_mix, dithers, patch_of, column_taps, row_taps
):
    extent = observed.shape[1]
    band, patches, _ = estimate.shape
    bases, tiles = blur_mix.shape[1:3]
    vmem = pl.BlockSpec(memory_space=pltpu.VMEM)
    smem = pl.BlockSpec(memory_space=pltpu.SMEM)
    in_specs = [smem, smem] + [vmem] * 6
    limit = 56 * 2**20
    planes = size // 4
    if size % 8 == 0 and planes & (planes - 1) == 0 and band % EDGE == 0:
        sems = [planes, planes, planes, planes, 2 * planes, 2 * planes] + [2 * planes] * 2 + [planes] * 4
        return pl.pallas_call(
            functools.partial(fused_kernel, size),
            out_shape=jax.ShapeDtypeStruct(estimate.shape, F32),
            in_specs=[smem, smem, vmem] + [pl.BlockSpec(memory_space=pl.ANY)] * 2 + [vmem] * 3,
            out_specs=vmem,
            scratch_shapes=work_shapes(bases, tiles, extent, extent // 2)
            + [
                pltpu.VMEM((patches, extent, extent), BF16),
                pltpu.VMEM((patches, extent, extent), BF16),
                pltpu.VMEM((2 * planes, patches, band, extent), BF16),
                pltpu.VMEM((planes, patches, band, extent), BF16),
                pltpu.VMEM((planes, patches, band, extent), BF16),
                pltpu.VMEM((planes, patches, band, extent), BF16),
                pltpu.VMEM((planes, patches, band, extent), BF16),
            ]
            + [pltpu.SemaphoreType.DMA((count,)) for count in sems]
            + [
                pltpu.VMEM((extent, extent), observed.dtype),
                pltpu.VMEM((extent, extent), pixel_mask.dtype),
                pltpu.SemaphoreType.DMA((2,)),
            ],
            compiler_params=pltpu.CompilerParams(
                collective_id=0, has_side_effects=True, vmem_limit_bytes=limit
            ),
        )(dithers, patch_of, estimate, observed, pixel_mask, blur_mix, column_taps, row_taps)

    low = jnp.transpose(estimate.astype(BF16), (1, 0, 2))
    gathered = lax.all_gather(low, "exp", axis=1, tiled=True)
    term = pl.pallas_call(
        local_kernel,
        out_shape=jax.ShapeDtypeStruct((patches, extent, extent), F32),
        in_specs=in_specs,
        out_specs=vmem,
        scratch_shapes=work_shapes(bases, tiles, extent, extent),
        compiler_params=pltpu.CompilerParams(vmem_limit_bytes=limit),
    )(dithers, patch_of, gathered, observed, pixel_mask, blur_mix, column_taps, row_taps)
    mine = lax.psum_scatter(term, "exp", scatter_dimension=1, tiled=True)
    return jnp.transpose(mine, (1, 0, 2))


def spread_mix(mix_ref, spread_ref):
    _, bases, tiles, _ = mix_ref.shape
    extent = spread_ref.shape[2]
    lane_tile = lax.broadcasted_iota(jnp.int32, (tiles, extent), 1) // (extent // tiles)
    for k in range(bases):
        weights = mix_ref[0, k]
        spread = jnp.zeros((tiles, extent), F32)
        for tile in range(tiles):
            spread = jnp.where(lane_tile == tile, weights[:, tile : tile + 1], spread)
        spread_ref[k] = spread


def mix_full(spread_ref, k):
    tiles, extent = spread_ref.shape[1:]
    weights = spread_ref[k]
    return jnp.broadcast_to(weights[:, None, :], (tiles, extent // tiles, extent)).reshape(
        extent, extent
    )


def solution(mesh):
    in_specs = (
        P("exp", "groups", None),
        P(("groups", "exp"), None, None),
        P(("groups", "exp"), None, None),
        P(("groups", "exp"), None, None, None),
        P(("groups", "exp"), None),
        P(("groups", "exp")),
        P(),
        P(),
    )
    return jax.shard_map(
        functools.partial(per_device, mesh.shape["exp"]),
        mesh=mesh,
        in_specs=in_specs,
        out_specs=P("exp", "groups", None),
        check_vma=False,
    )
```

```python
import functools

import jax
import jax.numpy as jnp
from jax import lax
from jax.experimental import pallas as pl
from jax.experimental.pallas import tpu as pltpu
from jax.sharding import PartitionSpec as P

BLOCK = 128
EDGE = 16
F32 = jnp.float32
BF16 = jnp.bfloat16


def dot(a, b):
    return jnp.dot(a, b, preferred_element_type=F32)


def build_bands(taps_ref, plain_ref, flipped_ref, shift):
    taps = taps_ref[...].astype(F32)
    bases, width = taps.shape
    half = width // 2
    extent = plain_ref.shape[1]
    blocks = extent // BLOCK
    zero = jnp.zeros((extent, extent), plain_ref.dtype)
    for k in range(bases):
        plain_ref[k] = zero
        flipped_ref[k] = zero

    top = (8, BLOCK)
    apart = lax.broadcasted_iota(jnp.int32, top, 0) - lax.broadcasted_iota(jnp.int32, top, 1)
    apart = jnp.where(apart < -BLOCK // 2, apart + BLOCK, apart)
    ahead = apart + (half - shift)
    behind = (half - shift) - apart
    row = lax.broadcasted_iota(jnp.int32, (BLOCK, BLOCK), 0)
    column = lax.broadcasted_iota(jnp.int32, (BLOCK, BLOCK), 1)
    wrapped_down = row - column < -BLOCK // 2
    wrapped_up = row - column > BLOCK // 2
    parts = (
        (0, BLOCK, 0, ~(wrapped_down | wrapped_up)),
        (0, EDGE, -1, wrapped_down),
        (BLOCK - EDGE, EDGE, 1, wrapped_up),
    )
    for k in range(bases):
        plain_top, flipped_top = jnp.zeros(top, F32), jnp.zeros(top, F32)
        for t in range(width):
            tap = taps[k : k + 1, t : t + 1]
            plain_top = jnp.where(ahead == t, tap, plain_top)
            flipped_top = jnp.where(behind == t, tap, flipped_top)

        def all_rows(rows_of):
            rolled = [rows_of] + [pltpu.roll(rows_of, g, 1) for g in range(8, BLOCK, 8)]
            return jnp.concatenate(rolled, axis=0)

        plain, flipped = all_rows(plain_top), all_rows(flipped_top)
        for first, rows, aside, kept in parts:
            stored = slice(first, first + rows)
            one = jnp.where(kept[stored], plain[stored], 0.0)
            two = jnp.where(kept[stored], flipped[stored], 0.0)
            for block in range(blocks):
                if not 0 <= block + aside < blocks:
                    continue
                source = row[stored] + (block * BLOCK - shift)
                target = column[stored] + ((block + aside) * BLOCK - shift)
                row_inside = (source >= 0) & (source < extent)
                column_inside = (target >= 0) & (target < extent)
                outer_row = block in (0, blocks - 1)
                outer_column = block + aside in (0, blocks - 1)
                at = (
                    k,
                    pl.ds(block * BLOCK + first, rows),
                    pl.ds((block + aside) * BLOCK, BLOCK),
                )
                inner_one = jnp.where(row_inside, one, 0.0) if outer_row else one
                inner_two = jnp.where(column_inside, two, 0.0) if outer_column else two
                plain_ref[at] = inner_one.astype(BF16)
                flipped_ref[at] = inner_two.astype(BF16)


def forward_residual(observed, mask, spread, column_flip, rowed, model):
    bases = spread.shape[0]
    model[...] = mix_full(spread, 0) * dot(column_flip[0], rowed[0])

    def basis(k, _):
        model[...] += mix_full(spread, k) * dot(column_flip[k], rowed[k])
        return 0

    lax.fori_loop(1, bases, basis, 0, unroll=True)
    model[...] = mask[...].astype(F32) * (model[...] - observed[...].astype(F32))


def backward(first, last, make, rows, spread, row_flip, column_band, model, weighted, total):
    def basis(k, _):
        if make:
            weighted[k] = (mix_full(spread, k) * model[...]).astype(BF16)
        backed = dot(column_band[k, rows, :], weighted[k]).astype(BF16)
        total[...] += dot(backed, row_flip[k])
        return 0

    lax.fori_loop(first, last, basis, 0, unroll=True)


def local_kernel(
    dithers, patch_of, estimate, observed, mask, mix, column_taps, row_taps, term,
    row_band, row_flip, column_band, column_flip, spread, weighted, model, total,
):
    extent = observed.shape[1]
    build_bands(row_taps, row_band, row_flip, dithers[0, 1])
    build_bands(column_taps, column_band, column_flip, dithers[0, 0])
    spread_mix(mix, spread)
    patch = patch_of[0]
    bases = spread.shape[0]
    for k in range(bases):
        weighted[k] = dot(estimate[patch], row_band[k]).astype(BF16)
    forward_residual(observed.at[0], mask.at[0], spread, column_flip, weighted, model)
    total[...] = jnp.zeros_like(total)
    everything = pl.ds(0, extent)
    backward(0, bases, True, everything, spread, row_flip, column_band, model, weighted, total)
    for q in range(term.shape[0]):
        term[q] = jnp.where(patch == q, total[...], 0.0)


def fused_kernel(
    size, dithers, patch_of, estimate, observed, mask, mix, column_taps, row_taps, out,
    row_band, row_flip, column_band, column_flip, spread, weighted, model, total,
    gathered, low, from_core, to_row, from_row, to_plane, from_plane,
    z_send, z_recv, y_send, y_recv, c_send, c_recv,
    rc_send, rc_recv, ry_send, ry_recv, rz_send, rz_recv, frame, good, load_sem,
):
    planes = size // 4
    band, patches, _ = estimate.shape
    extent = observed.shape[1]
    bases = spread.shape[0]
    me = lax.axis_index("exp")
    plane, y, core = me // 4, (me // 2) % 2, me % 2

    def index(p, yy, cc):
        return p * 4 + yy * 2 + cc

    def mirror(x):
        p, bit = 0, 1
        while bit < planes:
            p = p + ((plane // bit + x // bit) % 2) * bit
            bit *= 2
        return p

    other_core, other_row = index(plane, y, 1 - core), index(plane, 1 - y, core)

    def copy(source, target, send, recv, device):
        return pltpu.make_async_remote_copy(
            src_ref=source, dst_ref=target, send_sem=send, recv_sem=recv,
            device_id={"exp": device}, device_id_type=pl.DeviceIdType.MESH,
        )

    def shard(owner):
        return gathered.at[:, pl.ds(pl.multiple_of(owner * band, band), band), :]

    def rows_at(start, count):
        return pl.ds(pl.multiple_of(start, count), count)

    near, far = list(range(planes // 2)), list(range(planes // 2, planes))
    loads = [
        pltpu.make_async_copy(observed.at[0], frame, load_sem.at[0]),
        pltpu.make_async_copy(mask.at[0], good, load_sem.at[1]),
    ]
    barrier = pltpu.get_barrier_semaphore()
    partners = [other_core, other_row] + [index(mirror(d), y, core) for d in range(1, planes)]
    for partner in partners:
        pl.semaphore_signal(
            barrier, inc=1, device_id={"exp": partner}, device_id_type=pl.DeviceIdType.MESH
        )
    mine = rows_at(me * band, band)
    for q in range(patches):
        gathered[q, mine, :] = estimate[:, q, :].astype(BF16)
    pl.semaphore_wait(barrier, len(partners))

    def z_copy(d):
        return copy(shard(me), shard(me), z_send.at[d], z_recv.at[d], index(mirror(d), y, core))

    def y_copy(d):
        held = shard(index(mirror(d), y, core))
        return copy(held, held, y_send.at[d], y_recv.at[d], other_row)

    def c_copy(d, across):
        held = shard(index(mirror(d), (1 - y) if across else y, core))
        slot = d * 2 + across
        return copy(held, held, c_send.at[slot], c_recv.at[slot], other_core)

    y_copy(0).start()
    for d in far + near[1:]:
        z_copy(d).start()
    c_copy(0, 0).start()
    for load in loads:
        load.start()
    build_bands(row_taps, row_band, row_flip, dithers[0, 1])
    for d in range(1, planes):
        z_copy(d).wait_recv()
        y_copy(d).start()
        c_copy(d, 0).start()

    def forward_y(d):
        y_copy(d).wait_recv()
        c_copy(d, 1).start()

    def blur_rows(yy):
        starts = [p * 4 * band + yy * 2 * band for p in range(planes)]

        def of_patch(q):
            return jnp.concatenate(
                [gathered[q, rows_at(start, 2 * band), :] for start in starts], axis=0
            )

        joined = of_patch(0)
        for q in range(1, patches):
            joined = jnp.where(patch == q, of_patch(q), joined)
        for k in range(bases):
            rowed = dot(joined, row_band[k]).astype(BF16)
            for p in range(planes):
                piece_rows = rowed[p * 2 * band : (p + 1) * 2 * band]
                weighted[k, rows_at(starts[p], 2 * band), :] = piece_rows

    patch = patch_of[0]
    forward_y(0)
    build_bands(column_taps, column_band, column_flip, dithers[0, 0])
    spread_mix(mix, spread)
    forward_y(1)
    for d in range(planes):
        c_copy(d, 0).wait_recv()
    blur_rows(y)
    for d in range(2, planes):
        forward_y(d)
    for d in range(planes):
        c_copy(d, 1).wait_recv()
    for load in loads:
        load.wait()
    blur_rows(1 - y)
    forward_residual(frame, good, spread, column_flip, weighted, model)

    def owned(d, yy, cc):
        return rows_at(index(mirror(d), yy, cc) * band, band)

    def half_rows(planes_of):
        lowest = mirror(planes_of[0]) // len(planes_of) * len(planes_of)
        return rows_at(lowest * 4 * band, extent // 2)

    def rc_copy(d, across):
        slot = d * 2 + across
        rows = owned(d, (1 - y) if across else y, 1 - core)
        return copy(
            low.at[:, rows, :], from_core.at[slot], rc_send.at[slot], rc_recv.at[slot], other_core
        )

    def ry_copy(d):
        return copy(to_row.at[d], from_row.at[d], ry_send.at[d], ry_recv.at[d], other_row)

    def rz_copy(d):
        return copy(
            to_plane.at[d], from_plane.at[d], rz_send.at[d], rz_recv.at[d],
            index(mirror(d), y, core),
        )

    def back(first, last, make, planes_of):
        half = half_rows(planes_of)
        backward(first, last, make, half, spread, row_flip, column_band, model, weighted, total)

    def to_core(planes_of):
        half = half_rows(planes_of)
        for q in range(patches):
            low[q, half, :] = jnp.where(patch == q, total[...], 0.0).astype(BF16)
        for across in (1, 0):
            for d in planes_of:
                rc_copy(d, across).start()

    def core_sum(d, across, q):
        rows = owned(d, (1 - y) if across else y, core)
        return low[q, rows, :].astype(F32) + from_core[d * 2 + across, q].astype(F32)

    def to_other_row(planes_of):
        for d in planes_of:
            rc_copy(d, 1).wait_recv()
            for q in range(patches):
                to_row[d, q] = core_sum(d, 1, q).astype(BF16)
            ry_copy(d).start()

    def row_sum(d):
        rc_copy(d, 0).wait_recv()
        ry_copy(d).wait_recv()
        return [core_sum(d, 0, q) + from_row[d, q].astype(F32) for q in range(patches)]

    def to_other_plane(d):
        sums = row_sum(d)
        for q in range(patches):
            to_plane[d, q] = sums[q].astype(BF16)
        rz_copy(d).start()

    near_last = near[1:] + near[:1]
    total[...] = jnp.zeros_like(total)
    back(0, bases, True, far)
    to_core(far)
    total[...] = jnp.zeros_like(total)
    back(0, bases // 2, False, near)
    to_other_row(far)
    back(bases // 2, bases, False, near)
    to_core(near_last)
    to_other_plane(far[0])
    to_other_row(near_last)
    for d in far[1:] + near[1:]:
        to_other_plane(d)
    final = row_sum(0)
    for d in near[1:] + far:
        rz_copy(d).wait_recv()
        for q in range(patches):
            final[q] = final[q] + from_plane[d, q].astype(F32)
    for q in range(patches):
        out[:, q, :] = final[q]

    for d in range(planes):
        if d > 0:
            z_copy(d).wait_send()
            rz_copy(d).wait_send()
        y_copy(d).wait_send()
        c_copy(d, 0).wait_send()
        c_copy(d, 1).wait_send()
        ry_copy(d).wait_send()
        rc_copy(d, 0).wait_send()
        rc_copy(d, 1).wait_send()


def work_shapes(bases, tiles, extent, total_rows):
    return [pltpu.VMEM((bases, extent, extent), BF16) for _ in range(4)] + [
        pltpu.VMEM((bases, tiles, extent), F32),
        pltpu.VMEM((bases, extent, extent), BF16),
        pltpu.VMEM((extent, extent), F32),
        pltpu.VMEM((total_rows, extent), F32),
    ]


def per_device(
    size, estimate, observed, pixel_mask, blur_mix, dithers, patch_of, column_taps, row_taps
):
    extent = observed.shape[1]
    band, patches, _ = estimate.shape
    bases, tiles = blur_mix.shape[1:3]
    vmem = pl.BlockSpec(memory_space=pltpu.VMEM)
    smem = pl.BlockSpec(memory_space=pltpu.SMEM)
    in_specs = [smem, smem] + [vmem] * 6
    limit = 56 * 2**20
    planes = size // 4
    if size % 8 == 0 and planes & (planes - 1) == 0 and band % EDGE == 0:
        sems = [planes, planes, planes, planes, 2 * planes, 2 * planes] + [2 * planes] * 2 + [planes] * 4
        return pl.pallas_call(
            functools.partial(fused_kernel, size),
            out_shape=jax.ShapeDtypeStruct(estimate.shape, F32),
            in_specs=[smem, smem, vmem] + [pl.BlockSpec(memory_space=pl.ANY)] * 2 + [vmem] * 3,
            out_specs=vmem,
            scratch_shapes=work_shapes(bases, tiles, extent, extent // 2)
            + [
                pltpu.VMEM((patches, extent, extent), BF16),
                pltpu.VMEM((patches, extent, extent), BF16),
                pltpu.VMEM((2 * planes, patches, band, extent), BF16),
                pltpu.VMEM((planes, patches, band, extent), BF16),
                pltpu.VMEM((planes, patches, band, extent), BF16),
                pltpu.VMEM((planes, patches, band, extent), BF16),
                pltpu.VMEM((planes, patches, band, extent), BF16),
            ]
            + [pltpu.SemaphoreType.DMA((count,)) for count in sems]
            + [
                pltpu.VMEM((extent, extent), observed.dtype),
                pltpu.VMEM((extent, extent), pixel_mask.dtype),
                pltpu.SemaphoreType.DMA((2,)),
            ],
            compiler_params=pltpu.CompilerParams(
                collective_id=0, has_side_effects=True, vmem_limit_bytes=limit
            ),
        )(dithers, patch_of, estimate, observed, pixel_mask, blur_mix, column_taps, row_taps)

    low = jnp.transpose(estimate.astype(BF16), (1, 0, 2))
    gathered = lax.all_gather(low, "exp", axis=1, tiled=True)
    term = pl.pallas_call(
        local_kernel,
        out_shape=jax.ShapeDtypeStruct((patches, extent, extent), F32),
        in_specs=in_specs,
        out_specs=vmem,
        scratch_shapes=work_shapes(bases, tiles, extent, extent),
        compiler_params=pltpu.CompilerParams(vmem_limit_bytes=limit),
    )(dithers, patch_of, gathered, observed, pixel_mask, blur_mix, column_taps, row_taps)
    mine = lax.psum_scatter(term, "exp", scatter_dimension=1, tiled=True)
    return jnp.transpose(mine, (1, 0, 2))


def spread_mix(mix_ref, spread_ref):
    _, bases, tiles, _ = mix_ref.shape
    extent = spread_ref.shape[2]
    lane_tile = lax.broadcasted_iota(jnp.int32, (tiles, extent), 1) // (extent // tiles)
    for k in range(bases):
        weights = mix_ref[0, k]
        spread = jnp.zeros((tiles, extent), F32)
        for tile in range(tiles):
            spread = jnp.where(lane_tile == tile, weights[:, tile : tile + 1], spread)
        spread_ref[k] = spread


def mix_full(spread_ref, k):
    tiles, extent = spread_ref.shape[1:]
    weights = spread_ref[k]
    return jnp.broadcast_to(weights[:, None, :], (tiles, extent // tiles, extent)).reshape(
        extent, extent
    )


def solution(mesh):
    in_specs = (
        P("exp", "groups", None),
        P(("groups", "exp"), None, None),
        P(("groups", "exp"), None, None),
        P(("groups", "exp"), None, None, None),
        P(("groups", "exp"), None),
        P(("groups", "exp")),
        P(),
        P(),
    )
    return jax.shard_map(
        functools.partial(per_device, mesh.shape["exp"]),
        mesh=mesh,
        in_specs=in_specs,
        out_specs=P("exp", "groups", None),
        check_vma=False,
    )
```

```python
import functools

import jax
import jax.numpy as jnp
from jax import lax
from jax.experimental import pallas as pl
from jax.experimental.pallas import tpu as pltpu
from jax.sharding import PartitionSpec as P

BLOCK = 128
EDGE = 16
F32 = jnp.float32
BF16 = jnp.bfloat16


def dot(a, b):
    return jnp.dot(a, b, preferred_element_type=F32)


def build_bands(taps_ref, plain_ref, flipped_ref, shift):
    taps = taps_ref[...].astype(F32)
    bases, width = taps.shape
    half = width // 2
    extent = plain_ref.shape[1]
    blocks = extent // BLOCK
    zero = jnp.zeros((extent, extent), plain_ref.dtype)
    for k in range(bases):
        plain_ref[k] = zero
        flipped_ref[k] = zero

    top = (8, BLOCK)
    apart = lax.broadcasted_iota(jnp.int32, top, 0) - lax.broadcasted_iota(jnp.int32, top, 1)
    apart = jnp.where(apart < -BLOCK // 2, apart + BLOCK, apart)
    ahead = apart + (half - shift)
    behind = (half - shift) - apart
    row = lax.broadcasted_iota(jnp.int32, (BLOCK, BLOCK), 0)
    column = lax.broadcasted_iota(jnp.int32, (BLOCK, BLOCK), 1)
    wrapped_down = row - column < -BLOCK // 2
    wrapped_up = row - column > BLOCK // 2
    parts = (
        (0, BLOCK, 0, ~(wrapped_down | wrapped_up)),
        (0, EDGE, -1, wrapped_down),
        (BLOCK - EDGE, EDGE, 1, wrapped_up),
    )
    for k in range(bases):
        plain_top, flipped_top = jnp.zeros(top, F32), jnp.zeros(top, F32)
        for t in range(width):
            tap = taps[k : k + 1, t : t + 1]
            plain_top = jnp.where(ahead == t, tap, plain_top)
            flipped_top = jnp.where(behind == t, tap, flipped_top)

        def all_rows(rows_of):
            rolled = [rows_of] + [pltpu.roll(rows_of, g, 1) for g in range(8, BLOCK, 8)]
            return jnp.concatenate(rolled, axis=0)

        plain, flipped = all_rows(plain_top), all_rows(flipped_top)
        for first, rows, aside, kept in parts:
            stored = slice(first, first + rows)
            one = jnp.where(kept[stored], plain[stored], 0.0)
            two = jnp.where(kept[stored], flipped[stored], 0.0)
            for block in range(blocks):
                if not 0 <= block + aside < blocks:
                    continue
                source = row[stored] + (block * BLOCK - shift)
                target = column[stored] + ((block + aside) * BLOCK - shift)
                row_inside = (source >= 0) & (source < extent)
                column_inside = (target >= 0) & (target < extent)
                outer_row = block in (0, blocks - 1)
                outer_column = block + aside in (0, blocks - 1)
                at = (
                    k,
                    pl.ds(block * BLOCK + first, rows),
                    pl.ds((block + aside) * BLOCK, BLOCK),
                )
                inner_one = jnp.where(row_inside, one, 0.0) if outer_row else one
                inner_two = jnp.where(column_inside, two, 0.0) if outer_column else two
                plain_ref[at] = inner_one.astype(BF16)
                flipped_ref[at] = inner_two.astype(BF16)


def forward_residual(observed, mask, spread, column_flip, rowed, model):
    bases = spread.shape[0]
    model[...] = mix_full(spread, 0) * dot(column_flip[0], rowed[0])

    def basis(k, _):
        model[...] += mix_full(spread, k) * dot(column_flip[k], rowed[k])
        return 0

    lax.fori_loop(1, bases, basis, 0, unroll=True)
    model[...] = mask[...].astype(F32) * (model[...] - observed[...].astype(F32))


def backward(first, last, make, rows, spread, row_flip, column_band, model, weighted, total):
    def basis(k, _):
        if make:
            weighted[k] = (mix_full(spread, k) * model[...]).astype(BF16)
        backed = dot(column_band[k, rows, :], weighted[k]).astype(BF16)
        total[...] += dot(backed, row_flip[k])
        return 0

    lax.fori_loop(first, last, basis, 0, unroll=True)


def local_kernel(
    dithers, patch_of, estimate, observed, mask, mix, column_taps, row_taps, term,
    row_band, row_flip, column_band, column_flip, spread, weighted, model, total,
):
    extent = observed.shape[1]
    build_bands(row_taps, row_band, row_flip, dithers[0, 1])
    build_bands(column_taps, column_band, column_flip, dithers[0, 0])
    spread_mix(mix, spread)
    patch = patch_of[0]
    bases = spread.shape[0]
    for k in range(bases):
        weighted[k] = dot(estimate[patch], row_band[k]).astype(BF16)
    forward_residual(observed.at[0], mask.at[0], spread, column_flip, weighted, model)
    total[...] = jnp.zeros_like(total)
    everything = pl.ds(0, extent)
    backward(0, bases, True, everything, spread, row_flip, column_band, model, weighted, total)
    for q in range(term.shape[0]):
        term[q] = jnp.where(patch == q, total[...], 0.0)


def fused_kernel(
    size, dithers, patch_of, estimate, observed, mask, mix, column_taps, row_taps, out,
    row_band, row_flip, column_band, column_flip, spread, weighted, model, total,
    gathered, low, from_core, to_row, from_row, to_plane, from_plane,
    z_send, z_recv, y_send, y_recv, c_send, c_recv,
    rc_send, rc_recv, ry_send, ry_recv, rz_send, rz_recv, frame, good, load_sem,
):
    planes = size // 4
    band, patches, _ = estimate.shape
    extent = observed.shape[1]
    bases = spread.shape[0]
    me = lax.axis_index("exp")
    plane, y, core = me // 4, (me // 2) % 2, me % 2

    def index(p, yy, cc):
        return p * 4 + yy * 2 + cc

    def mirror(x):
        p, bit = 0, 1
        while bit < planes:
            p = p + ((plane // bit + x // bit) % 2) * bit
            bit *= 2
        return p

    other_core, other_row = index(plane, y, 1 - core), index(plane, 1 - y, core)

    def copy(source, target, send, recv, device):
        return pltpu.make_async_remote_copy(
            src_ref=source, dst_ref=target, send_sem=send, recv_sem=recv,
            device_id={"exp": device}, device_id_type=pl.DeviceIdType.MESH,
        )

    def shard(owner):
        return gathered.at[:, pl.ds(pl.multiple_of(owner * band, band), band), :]

    def rows_at(start, count):
        return pl.ds(pl.multiple_of(start, count), count)

    near, far = list(range(planes // 2)), list(range(planes // 2, planes))
    loads = [
        pltpu.make_async_copy(observed.at[0], frame, load_sem.at[0]),
        pltpu.make_async_copy(mask.at[0], good, load_sem.at[1]),
    ]
    relayed = 3 if planes == 4 else None
    direct = [d for d in far + near[1:] if d != relayed]
    barrier = pltpu.get_barrier_semaphore()
    partners = [other_core, other_row] + [index(mirror(d), y, core) for d in direct]
    for partner in partners:
        pl.semaphore_signal(
            barrier, inc=1, device_id={"exp": partner}, device_id_type=pl.DeviceIdType.MESH
        )
    mine = rows_at(me * band, band)
    for q in range(patches):
        gathered[q, mine, :] = estimate[:, q, :].astype(BF16)
    pl.semaphore_wait(barrier, len(partners))

    def z_copy(d):
        held = shard(index(mirror(2), y, core) if d == relayed else me)
        to = index(mirror(1 if d == relayed else d), y, core)
        return copy(held, held, z_send.at[d], z_recv.at[d], to)

    def y_copy(d):
        held = shard(index(mirror(d), y, core))
        return copy(held, held, y_send.at[d], y_recv.at[d], other_row)

    def c_copy(d, across):
        held = shard(index(mirror(d), (1 - y) if across else y, core))
        slot = d * 2 + across
        return copy(held, held, c_send.at[slot], c_recv.at[slot], other_core)

    y_copy(0).start()
    for d in direct:
        z_copy(d).start()
    c_copy(0, 0).start()
    for load in loads:
        load.start()
    build_bands(row_taps, row_band, row_flip, dithers[0, 1])
    for d in direct:
        z_copy(d).wait_recv()
        if relayed and d == 2:
            z_copy(relayed).start()
        y_copy(d).start()
        c_copy(d, 0).start()

    def forward_y(d):
        y_copy(d).wait_recv()
        c_copy(d, 1).start()

    def blur_rows(yy):
        starts = [p * 4 * band + yy * 2 * band for p in range(planes)]

        def of_patch(q):
            return jnp.concatenate(
                [gathered[q, rows_at(start, 2 * band), :] for start in starts], axis=0
            )

        joined = of_patch(0)
        for q in range(1, patches):
            joined = jnp.where(patch == q, of_patch(q), joined)
        for k in range(bases):
            rowed = dot(joined, row_band[k]).astype(BF16)
            for p in range(planes):
                piece_rows = rowed[p * 2 * band : (p + 1) * 2 * band]
                weighted[k, rows_at(starts[p], 2 * band), :] = piece_rows

    patch = patch_of[0]
    forward_y(0)
    build_bands(column_taps, column_band, column_flip, dithers[0, 0])
    spread_mix(mix, spread)
    if relayed:
        z_copy(relayed).wait_recv()
        y_copy(relayed).start()
        c_copy(relayed, 0).start()
    forward_y(1)
    for d in range(planes):
        c_copy(d, 0).wait_recv()
    blur_rows(y)
    for d in range(2, planes):
        forward_y(d)
    for d in range(planes):
        c_copy(d, 1).wait_recv()
    for load in loads:
        load.wait()
    blur_rows(1 - y)
    forward_residual(frame, good, spread, column_flip, weighted, model)

    def owned(d, yy, cc):
        return rows_at(index(mirror(d), yy, cc) * band, band)

    def half_rows(planes_of):
        lowest = mirror(planes_of[0]) // len(planes_of) * len(planes_of)
        return rows_at(lowest * 4 * band, extent // 2)

    def rc_copy(d, across):
        slot = d * 2 + across
        rows = owned(d, (1 - y) if across else y, 1 - core)
        return copy(
            low.at[:, rows, :], from_core.at[slot], rc_send.at[slot], rc_recv.at[slot], other_core
        )

    def ry_copy(d):
        return copy(to_row.at[d], from_row.at[d], ry_send.at[d], ry_recv.at[d], other_row)

    def rz_copy(d):
        return copy(
            to_plane.at[d], from_plane.at[d], rz_send.at[d], rz_recv.at[d],
            index(mirror(1 if d == relayed else d), y, core),
        )

    def back(first, last, make, planes_of):
        half = half_rows(planes_of)
        backward(first, last, make, half, spread, row_flip, column_band, model, weighted, total)

    def to_core(planes_of):
        half = half_rows(planes_of)
        for q in range(patches):
            low[q, half, :] = jnp.where(patch == q, total[...], 0.0).astype(BF16)
        for across in (1, 0):
            for d in planes_of:
                rc_copy(d, across).start()

    def core_sum(d, across, q):
        rows = owned(d, (1 - y) if across else y, core)
        return low[q, rows, :].astype(F32) + from_core[d * 2 + across, q].astype(F32)

    def to_other_row(planes_of):
        for d in planes_of:
            rc_copy(d, 1).wait_recv()
            for q in range(patches):
                to_row[d, q] = core_sum(d, 1, q).astype(BF16)
            ry_copy(d).start()

    def row_sum(d):
        rc_copy(d, 0).wait_recv()
        ry_copy(d).wait_recv()
        return [core_sum(d, 0, q) + from_row[d, q].astype(F32) for q in range(patches)]

    def to_other_plane(d):
        sums = row_sum(d)
        if relayed and d == 2:
            rz_copy(relayed).wait_recv()
            sums = [sums[q] + from_plane[relayed, q].astype(F32) for q in range(patches)]
        for q in range(patches):
            to_plane[d, q] = sums[q].astype(BF16)
        rz_copy(d).start()

    near_last = near[1:] + near[:1]
    far = far[::-1]
    total[...] = jnp.zeros_like(total)
    back(0, bases, True, far)
    to_core(far)
    total[...] = jnp.zeros_like(total)
    back(0, bases // 2, False, near)
    to_other_row(far)
    back(bases // 2, bases, False, near)
    to_core(near_last)
    to_other_plane(far[0])
    to_other_row(near_last)
    for d in far[1:] + near[1:]:
        to_other_plane(d)
    final = row_sum(0)
    for d in direct:
        rz_copy(d).wait_recv()
        for q in range(patches):
            final[q] = final[q] + from_plane[d, q].astype(F32)
    for q in range(patches):
        out[:, q, :] = final[q]

    for d in range(planes):
        if d > 0:
            z_copy(d).wait_send()
            rz_copy(d).wait_send()
        y_copy(d).wait_send()
        c_copy(d, 0).wait_send()
        c_copy(d, 1).wait_send()
        ry_copy(d).wait_send()
        rc_copy(d, 0).wait_send()
        rc_copy(d, 1).wait_send()


def work_shapes(bases, tiles, extent, total_rows):
    return [pltpu.VMEM((bases, extent, extent), BF16) for _ in range(4)] + [
        pltpu.VMEM((bases, tiles, extent), F32),
        pltpu.VMEM((bases, extent, extent), BF16),
        pltpu.VMEM((extent, extent), F32),
        pltpu.VMEM((total_rows, extent), F32),
    ]


def per_device(
    size, estimate, observed, pixel_mask, blur_mix, dithers, patch_of, column_taps, row_taps
):
    extent = observed.shape[1]
    band, patches, _ = estimate.shape
    bases, tiles = blur_mix.shape[1:3]
    vmem = pl.BlockSpec(memory_space=pltpu.VMEM)
    smem = pl.BlockSpec(memory_space=pltpu.SMEM)
    in_specs = [smem, smem] + [vmem] * 6
    limit = 56 * 2**20
    planes = size // 4
    if size % 8 == 0 and planes & (planes - 1) == 0 and band % EDGE == 0:
        sems = [planes, planes, planes, planes, 2 * planes, 2 * planes] + [2 * planes] * 2 + [planes] * 4
        return pl.pallas_call(
            functools.partial(fused_kernel, size),
            out_shape=jax.ShapeDtypeStruct(estimate.shape, F32),
            in_specs=[smem, smem, vmem] + [pl.BlockSpec(memory_space=pl.ANY)] * 2 + [vmem] * 3,
            out_specs=vmem,
            scratch_shapes=work_shapes(bases, tiles, extent, extent // 2)
            + [
                pltpu.VMEM((patches, extent, extent), BF16),
                pltpu.VMEM((patches, extent, extent), BF16),
                pltpu.VMEM((2 * planes, patches, band, extent), BF16),
                pltpu.VMEM((planes, patches, band, extent), BF16),
                pltpu.VMEM((planes, patches, band, extent), BF16),
                pltpu.VMEM((planes, patches, band, extent), BF16),
                pltpu.VMEM((planes, patches, band, extent), BF16),
            ]
            + [pltpu.SemaphoreType.DMA((count,)) for count in sems]
            + [
                pltpu.VMEM((extent, extent), observed.dtype),
                pltpu.VMEM((extent, extent), pixel_mask.dtype),
                pltpu.SemaphoreType.DMA((2,)),
            ],
            compiler_params=pltpu.CompilerParams(
                collective_id=0, has_side_effects=True, vmem_limit_bytes=limit
            ),
        )(dithers, patch_of, estimate, observed, pixel_mask, blur_mix, column_taps, row_taps)

    low = jnp.transpose(estimate.astype(BF16), (1, 0, 2))
    gathered = lax.all_gather(low, "exp", axis=1, tiled=True)
    term = pl.pallas_call(
        local_kernel,
        out_shape=jax.ShapeDtypeStruct((patches, extent, extent), F32),
        in_specs=in_specs,
        out_specs=vmem,
        scratch_shapes=work_shapes(bases, tiles, extent, extent),
        compiler_params=pltpu.CompilerParams(vmem_limit_bytes=limit),
    )(dithers, patch_of, gathered, observed, pixel_mask, blur_mix, column_taps, row_taps)
    mine = lax.psum_scatter(term, "exp", scatter_dimension=1, tiled=True)
    return jnp.transpose(mine, (1, 0, 2))


def spread_mix(mix_ref, spread_ref):
    _, bases, tiles, _ = mix_ref.shape
    extent = spread_ref.shape[2]
    lane_tile = lax.broadcasted_iota(jnp.int32, (tiles, extent), 1) // (extent // tiles)
    for k in range(bases):
        weights = mix_ref[0, k]
        spread = jnp.zeros((tiles, extent), F32)
        for tile in range(tiles):
            spread = jnp.where(lane_tile == tile, weights[:, tile : tile + 1], spread)
        spread_ref[k] = spread


def mix_full(spread_ref, k):
    tiles, extent = spread_ref.shape[1:]
    weights = spread_ref[k]
    return jnp.broadcast_to(weights[:, None, :], (tiles, extent // tiles, extent)).reshape(
        extent, extent
    )


def solution(mesh):
    in_specs = (
        P("exp", "groups", None),
        P(("groups", "exp"), None, None),
        P(("groups", "exp"), None, None),
        P(("groups", "exp"), None, None, None),
        P(("groups", "exp"), None),
        P(("groups", "exp")),
        P(),
        P(),
    )
    return jax.shard_map(
        functools.partial(per_device, mesh.shape["exp"]),
        mesh=mesh,
        in_specs=in_specs,
        out_specs=P("exp", "groups", None),
        check_vma=False,
    )
```

```python
import functools

import jax
import jax.numpy as jnp
from jax import lax
from jax.experimental import pallas as pl
from jax.experimental.pallas import tpu as pltpu
from jax.sharding import PartitionSpec as P

BLOCK = 128
EDGE = 16
F32 = jnp.float32
BF16 = jnp.bfloat16


def dot(a, b):
    return jnp.dot(a, b, preferred_element_type=F32)


def build_bands(taps_ref, plain_ref, flipped_ref, shift):
    taps = taps_ref[...].astype(F32)
    bases, width = taps.shape
    half = width // 2
    extent = plain_ref.shape[1]
    blocks = extent // BLOCK
    zero = jnp.zeros((extent, extent), plain_ref.dtype)
    for k in range(bases):
        plain_ref[k] = zero
        flipped_ref[k] = zero

    top = (8, BLOCK)
    apart = lax.broadcasted_iota(jnp.int32, top, 0) - lax.broadcasted_iota(jnp.int32, top, 1)
    apart = jnp.where(apart < -BLOCK // 2, apart + BLOCK, apart)
    ahead = apart + (half - shift)
    behind = (half - shift) - apart
    row = lax.broadcasted_iota(jnp.int32, (BLOCK, BLOCK), 0)
    column = lax.broadcasted_iota(jnp.int32, (BLOCK, BLOCK), 1)
    wrapped_down = row - column < -BLOCK // 2
    wrapped_up = row - column > BLOCK // 2
    parts = (
        (0, BLOCK, 0, ~(wrapped_down | wrapped_up)),
        (0, EDGE, -1, wrapped_down),
        (BLOCK - EDGE, EDGE, 1, wrapped_up),
    )
    for k in range(bases):
        plain_top, flipped_top = jnp.zeros(top, F32), jnp.zeros(top, F32)
        for t in range(width):
            tap = taps[k : k + 1, t : t + 1]
            plain_top = jnp.where(ahead == t, tap, plain_top)
            flipped_top = jnp.where(behind == t, tap, flipped_top)

        def all_rows(rows_of):
            rolled = [rows_of] + [pltpu.roll(rows_of, g, 1) for g in range(8, BLOCK, 8)]
            return jnp.concatenate(rolled, axis=0)

        plain, flipped = all_rows(plain_top), all_rows(flipped_top)
        for first, rows, aside, kept in parts:
            stored = slice(first, first + rows)
            one = jnp.where(kept[stored], plain[stored], 0.0)
            two = jnp.where(kept[stored], flipped[stored], 0.0)
            for block in range(blocks):
                if not 0 <= block + aside < blocks:
                    continue
                source = row[stored] + (block * BLOCK - shift)
                target = column[stored] + ((block + aside) * BLOCK - shift)
                row_inside = (source >= 0) & (source < extent)
                column_inside = (target >= 0) & (target < extent)
                outer_row = block in (0, blocks - 1)
                outer_column = block + aside in (0, blocks - 1)
                at = (
                    k,
                    pl.ds(block * BLOCK + first, rows),
                    pl.ds((block + aside) * BLOCK, BLOCK),
                )
                inner_one = jnp.where(row_inside, one, 0.0) if outer_row else one
                inner_two = jnp.where(column_inside, two, 0.0) if outer_column else two
                plain_ref[at] = inner_one.astype(BF16)
                flipped_ref[at] = inner_two.astype(BF16)


def forward_residual(observed, mask, spread, column_flip, rowed, model):
    bases = spread.shape[0]
    model[...] = mix_full(spread, 0) * dot(column_flip[0], rowed[0])

    def basis(k, _):
        model[...] += mix_full(spread, k) * dot(column_flip[k], rowed[k])
        return 0

    lax.fori_loop(1, bases, basis, 0, unroll=True)
    model[...] = mask[...].astype(F32) * (model[...] - observed[...].astype(F32))


def backward(first, last, make, rows, spread, row_flip, column_band, model, weighted, total):
    backed = []
    for k in range(first, last):
        if make:
            weighted[k] = (mix_full(spread, k) * model[...]).astype(BF16)
        backed.append(dot(column_band[k, rows, :], weighted[k]).astype(BF16))
    extent = row_flip.shape[2]
    stack = row_flip[first:last].reshape((last - first) * extent, extent)
    result = dot(jnp.concatenate(backed, axis=1), stack)
    total[...] = result if first == 0 else total[...] + result


def local_kernel(
    dithers, patch_of, estimate, observed, mask, mix, column_taps, row_taps, term,
    row_band, row_flip, column_band, column_flip, spread, weighted, model, total,
):
    extent = observed.shape[1]
    build_bands(row_taps, row_band, row_flip, dithers[0, 1])
    build_bands(column_taps, column_band, column_flip, dithers[0, 0])
    spread_mix(mix, spread)
    patch = patch_of[0]
    bases = spread.shape[0]
    for k in range(bases):
        weighted[k] = dot(estimate[patch], row_band[k]).astype(BF16)
    forward_residual(observed.at[0], mask.at[0], spread, column_flip, weighted, model)
    everything = pl.ds(0, extent)
    backward(0, bases, True, everything, spread, row_flip, column_band, model, weighted, total)
    for q in range(term.shape[0]):
        term[q] = jnp.where(patch == q, total[...], 0.0)


def fused_kernel(
    size, dithers, patch_of, estimate, observed, mask, mix, column_taps, row_taps, out,
    row_band, row_flip, column_band, column_flip, spread, weighted, model, total,
    gathered, low, from_core, to_row, from_row, to_plane, from_plane,
    z_send, z_recv, y_send, y_recv, c_send, c_recv,
    rc_send, rc_recv, ry_send, ry_recv, rz_send, rz_recv, frame, good, load_sem,
):
    planes = size // 4
    band, patches, _ = estimate.shape
    extent = observed.shape[1]
    bases = spread.shape[0]
    me = lax.axis_index("exp")
    plane, y, core = me // 4, (me // 2) % 2, me % 2

    def index(p, yy, cc):
        return p * 4 + yy * 2 + cc

    def mirror(x):
        p, bit = 0, 1
        while bit < planes:
            p = p + ((plane // bit + x // bit) % 2) * bit
            bit *= 2
        return p

    other_core, other_row = index(plane, y, 1 - core), index(plane, 1 - y, core)

    def copy(source, target, send, recv, device):
        return pltpu.make_async_remote_copy(
            src_ref=source, dst_ref=target, send_sem=send, recv_sem=recv,
            device_id={"exp": device}, device_id_type=pl.DeviceIdType.MESH,
        )

    def shard(owner):
        return gathered.at[:, pl.ds(pl.multiple_of(owner * band, band), band), :]

    def rows_at(start, count):
        return pl.ds(pl.multiple_of(start, count), count)

    near, far = list(range(planes // 2)), list(range(planes // 2, planes))
    loads = [
        pltpu.make_async_copy(observed.at[0], frame, load_sem.at[0]),
        pltpu.make_async_copy(mask.at[0], good, load_sem.at[1]),
    ]
    barrier = pltpu.get_barrier_semaphore()
    partners = [other_core, other_row] + [index(mirror(d), y, core) for d in range(1, planes)]
    for partner in partners:
        pl.semaphore_signal(
            barrier, inc=1, device_id={"exp": partner}, device_id_type=pl.DeviceIdType.MESH
        )
    mine = rows_at(me * band, band)
    for q in range(patches):
        gathered[q, mine, :] = estimate[:, q, :].astype(BF16)
    pl.semaphore_wait(barrier, len(partners))

    def z_copy(d):
        return copy(shard(me), shard(me), z_send.at[d], z_recv.at[d], index(mirror(d), y, core))

    def y_copy(d):
        held = shard(index(mirror(d), y, core))
        return copy(held, held, y_send.at[d], y_recv.at[d], other_row)

    def c_copy(d, across):
        held = shard(index(mirror(d), (1 - y) if across else y, core))
        slot = d * 2 + across
        return copy(held, held, c_send.at[slot], c_recv.at[slot], other_core)

    y_copy(0).start()
    for d in far + near[1:]:
        z_copy(d).start()
    c_copy(0, 0).start()
    for load in loads:
        load.start()
    build_bands(row_taps, row_band, row_flip, dithers[0, 1])
    for d in range(1, planes):
        z_copy(d).wait_recv()
        y_copy(d).start()
        c_copy(d, 0).start()

    def forward_y(d):
        y_copy(d).wait_recv()
        c_copy(d, 1).start()

    def blur_rows(yy):
        starts = [p * 4 * band + yy * 2 * band for p in range(planes)]

        def of_patch(q):
            return jnp.concatenate(
                [gathered[q, rows_at(start, 2 * band), :] for start in starts], axis=0
            )

        joined = of_patch(0)
        for q in range(1, patches):
            joined = jnp.where(patch == q, of_patch(q), joined)
        for k in range(bases):
            rowed = dot(joined, row_band[k]).astype(BF16)
            for p in range(planes):
                piece_rows = rowed[p * 2 * band : (p + 1) * 2 * band]
                weighted[k, rows_at(starts[p], 2 * band), :] = piece_rows

    patch = patch_of[0]
    forward_y(0)
    build_bands(column_taps, column_band, column_flip, dithers[0, 0])
    spread_mix(mix, spread)
    forward_y(1)
    for d in range(planes):
        c_copy(d, 0).wait_recv()
    blur_rows(y)
    for d in range(2, planes):
        forward_y(d)
    for d in range(planes):
        c_copy(d, 1).wait_recv()
    for load in loads:
        load.wait()
    blur_rows(1 - y)
    forward_residual(frame, good, spread, column_flip, weighted, model)

    def owned(d, yy, cc):
        return rows_at(index(mirror(d), yy, cc) * band, band)

    def half_rows(planes_of):
        lowest = mirror(planes_of[0]) // len(planes_of) * len(planes_of)
        return rows_at(lowest * 4 * band, extent // 2)

    def rc_copy(d, across):
        slot = d * 2 + across
        rows = owned(d, (1 - y) if across else y, 1 - core)
        return copy(
            low.at[:, rows, :], from_core.at[slot], rc_send.at[slot], rc_recv.at[slot], other_core
        )

    def ry_copy(d):
        return copy(to_row.at[d], from_row.at[d], ry_send.at[d], ry_recv.at[d], other_row)

    def rz_copy(d):
        return copy(
            to_plane.at[d], from_plane.at[d], rz_send.at[d], rz_recv.at[d],
            index(mirror(d), y, core),
        )

    def back(first, last, make, planes_of):
        half = half_rows(planes_of)
        backward(first, last, make, half, spread, row_flip, column_band, model, weighted, total)

    def to_core(planes_of):
        half = half_rows(planes_of)
        for q in range(patches):
            low[q, half, :] = jnp.where(patch == q, total[...], 0.0).astype(BF16)
        for across in (1, 0):
            for d in planes_of:
                rc_copy(d, across).start()

    def core_sum(d, across, q):
        rows = owned(d, (1 - y) if across else y, core)
        return low[q, rows, :].astype(F32) + from_core[d * 2 + across, q].astype(F32)

    def to_other_row(planes_of):
        for d in planes_of:
            rc_copy(d, 1).wait_recv()
            for q in range(patches):
                to_row[d, q] = core_sum(d, 1, q).astype(BF16)
            ry_copy(d).start()

    def row_sum(d):
        rc_copy(d, 0).wait_recv()
        ry_copy(d).wait_recv()
        return [core_sum(d, 0, q) + from_row[d, q].astype(F32) for q in range(patches)]

    def to_other_plane(d):
        sums = row_sum(d)
        for q in range(patches):
            to_plane[d, q] = sums[q].astype(BF16)
        rz_copy(d).start()

    near_last = near[1:] + near[:1]
    back(0, bases, True, far)
    to_core(far)
    back(0, bases // 2, False, near)
    to_other_row(far)
    back(bases // 2, bases, False, near)
    to_core(near_last)
    to_other_plane(far[0])
    to_other_row(near_last)
    for d in far[1:] + near[1:]:
        to_other_plane(d)
    final = row_sum(0)
    for d in near[1:] + far:
        rz_copy(d).wait_recv()
        for q in range(patches):
            final[q] = final[q] + from_plane[d, q].astype(F32)
    for q in range(patches):
        out[:, q, :] = final[q]

    for d in range(planes):
        if d > 0:
            z_copy(d).wait_send()
            rz_copy(d).wait_send()
        y_copy(d).wait_send()
        c_copy(d, 0).wait_send()
        c_copy(d, 1).wait_send()
        ry_copy(d).wait_send()
        rc_copy(d, 0).wait_send()
        rc_copy(d, 1).wait_send()


def work_shapes(bases, tiles, extent, total_rows):
    return [pltpu.VMEM((bases, extent, extent), BF16) for _ in range(4)] + [
        pltpu.VMEM((bases, tiles, extent), F32),
        pltpu.VMEM((bases, extent, extent), BF16),
        pltpu.VMEM((extent, extent), F32),
        pltpu.VMEM((total_rows, extent), F32),
    ]


def per_device(
    size, estimate, observed, pixel_mask, blur_mix, dithers, patch_of, column_taps, row_taps
):
    extent = observed.shape[1]
    band, patches, _ = estimate.shape
    bases, tiles = blur_mix.shape[1:3]
    vmem = pl.BlockSpec(memory_space=pltpu.VMEM)
    smem = pl.BlockSpec(memory_space=pltpu.SMEM)
    in_specs = [smem, smem] + [vmem] * 6
    limit = 56 * 2**20
    planes = size // 4
    if size % 8 == 0 and planes & (planes - 1) == 0 and band % EDGE == 0:
        sems = [planes, planes, planes, planes, 2 * planes, 2 * planes] + [2 * planes] * 2 + [planes] * 4
        return pl.pallas_call(
            functools.partial(fused_kernel, size),
            out_shape=jax.ShapeDtypeStruct(estimate.shape, F32),
            in_specs=[smem, smem, vmem] + [pl.BlockSpec(memory_space=pl.ANY)] * 2 + [vmem] * 3,
            out_specs=vmem,
            scratch_shapes=work_shapes(bases, tiles, extent, extent // 2)
            + [
                pltpu.VMEM((patches, extent, extent), BF16),
                pltpu.VMEM((patches, extent, extent), BF16),
                pltpu.VMEM((2 * planes, patches, band, extent), BF16),
                pltpu.VMEM((planes, patches, band, extent), BF16),
                pltpu.VMEM((planes, patches, band, extent), BF16),
                pltpu.VMEM((planes, patches, band, extent), BF16),
                pltpu.VMEM((planes, patches, band, extent), BF16),
            ]
            + [pltpu.SemaphoreType.DMA((count,)) for count in sems]
            + [
                pltpu.VMEM((extent, extent), observed.dtype),
                pltpu.VMEM((extent, extent), pixel_mask.dtype),
                pltpu.SemaphoreType.DMA((2,)),
            ],
            compiler_params=pltpu.CompilerParams(
                collective_id=0, has_side_effects=True, vmem_limit_bytes=limit
            ),
        )(dithers, patch_of, estimate, observed, pixel_mask, blur_mix, column_taps, row_taps)

    low = jnp.transpose(estimate.astype(BF16), (1, 0, 2))
    gathered = lax.all_gather(low, "exp", axis=1, tiled=True)
    term = pl.pallas_call(
        local_kernel,
        out_shape=jax.ShapeDtypeStruct((patches, extent, extent), F32),
        in_specs=in_specs,
        out_specs=vmem,
        scratch_shapes=work_shapes(bases, tiles, extent, extent),
        compiler_params=pltpu.CompilerParams(vmem_limit_bytes=limit),
    )(dithers, patch_of, gathered, observed, pixel_mask, blur_mix, column_taps, row_taps)
    mine = lax.psum_scatter(term, "exp", scatter_dimension=1, tiled=True)
    return jnp.transpose(mine, (1, 0, 2))


def spread_mix(mix_ref, spread_ref):
    _, bases, tiles, _ = mix_ref.shape
    extent = spread_ref.shape[2]
    lane_tile = lax.broadcasted_iota(jnp.int32, (tiles, extent), 1) // (extent // tiles)
    for k in range(bases):
        weights = mix_ref[0, k]
        spread = jnp.zeros((tiles, extent), F32)
        for tile in range(tiles):
            spread = jnp.where(lane_tile == tile, weights[:, tile : tile + 1], spread)
        spread_ref[k] = spread


def mix_full(spread_ref, k):
    tiles, extent = spread_ref.shape[1:]
    weights = spread_ref[k]
    return jnp.broadcast_to(weights[:, None, :], (tiles, extent // tiles, extent)).reshape(
        extent, extent
    )


def solution(mesh):
    in_specs = (
        P("exp", "groups", None),
        P(("groups", "exp"), None, None),
        P(("groups", "exp"), None, None),
        P(("groups", "exp"), None, None, None),
        P(("groups", "exp"), None),
        P(("groups", "exp")),
        P(),
        P(),
    )
    return jax.shard_map(
        functools.partial(per_device, mesh.shape["exp"]),
        mesh=mesh,
        in_specs=in_specs,
        out_specs=P("exp", "groups", None),
        check_vma=False,
    )
```
